32 devices in a mesh: dp: 4 (over y, x), rad: 4 (over z), azi: 2 (over core).
Axes of the slice: x: 2, y: 2, z: 4, core: 2. Of those that a mesh axis runs over, the one named last changes fastest.
Arguments:
- inputs: bfloat16 [4, 96, 16, 16, 256], P('dp', None, 'rad', 'azi'), may hold values from -6 to 6
- weight: bfloat16 [96, 2592], P('dp'), may hold values from -0.125 to 0.125
- bias: bfloat16 [96], P('dp'), may hold values from -3 to 3
- cotangent: bfloat16 [4, 96, 16, 16, 256], P('dp', None, 'rad', 'azi'), may hold values from -6 to 6
Outputs:
- output: bfloat16 [4, 96, 16, 16, 256], P('dp', None, 'rad', 'azi')
- input_grad: bfloat16 [4, 96, 16, 16, 256], P('dp', None, 'rad', 'azi')
- weight_grad: float32 [96, 2592], P('dp')
- bias_grad: float32 [96], P('dp')
The draws below stay inside these ranges and needn't reach their ends.
All inputs are finite; a program needn't handle non-finite values.
Results may differ from the reference program's by a relative error of at most 0.015.
Values may be sent and summed in bfloat16 or wider, within the bound.
A program may use at most 128 MiB of HBM per device.

```python
import jax
import jax.numpy as jnp
from jax import lax

C = 96
TAPS = 27
NA = 256
BATCH = 4
NR = 16
NT = 16


def shard_levels(key, extent, cuts, low, top_value):
    def one(dim, shards_of):
        steps = jax.random.uniform(jax.random.fold_in(jax.random.fold_in(key, 6), dim), (shards_of,), jnp.float32, low / len(cuts), top_value / len(cuts))
        return jnp.repeat(jnp.exp(steps), extent[dim] // shards_of).reshape((-1,) + (1,) * (len(extent) - dim - 1))

    factor_of = one(*cuts[0])
    for cut in cuts[1:]:
        factor_of = factor_of * one(*cut)
    return factor_of


def noise(key, extent, scale, bound, shards=(), dtype=jnp.bfloat16):
    array = scale * jax.random.normal(key, extent, jnp.float32)
    if shards:
        array = array * shard_levels(key, extent, shards, -0.22, 0.18)
    return jnp.clip(array, -bound, bound).astype(dtype)


def setup_inputs(seed: int = 0) -> dict:
    splits = jax.random.split(jax.random.key(seed), 5)
    return {
        "inputs": noise(splits[0], (BATCH, C, NR, NT, NA), 1.0, 6.0, ((0, 4), (2, 4), (3, 2))),
        "weight": noise(splits[1], (C, TAPS * C), (TAPS * C) ** -0.5, 0.125, ((0, 4),)),
        "bias": noise(splits[2], (C,), 0.5, 3.0, ((0, 4),)),
        "cotangent": noise(splits[3], (BATCH, C, NR, NT, NA), 1.0, 6.0, ((0, 4), (2, 4), (3, 2))),
    }


inverse_scale = 1.0 / 1024.0


def pad_field(field):
    field = jnp.pad(field, ((0, 0), (1, 1), (0, 0), (1, 1)))
    return jnp.concatenate([field[:, :, -1:], field, field[:, :, :1]], axis=2)


def stack_taps(padded, rad_off, azi_off, flipped):
    radial = padded.shape[1] - 2
    azimuth = padded.shape[2] - 2
    axial = padded.shape[3] - 2
    pieces = []
    for tap_k in range(3):
        start_a = 2 - tap_k if flipped else tap_k
        pieces.append(padded[:, rad_off:rad_off + radial, azi_off:azi_off + azimuth, start_a:start_a + axial])
    return jnp.concatenate(pieces, axis=0).astype(jnp.float32)


def reference(inputs, weight, bias, cotangent):
    channels = inputs.shape[1]
    out_rows = weight.shape[0]
    weight_f = weight.astype(jnp.float32)
    high = lax.Precision.HIGHEST

    def per_sample(pair_args):
        sample_in, sample_grad = pair_args
        padded = pad_field(sample_in)
        preact = jnp.zeros((out_rows,) + sample_in.shape[1:], jnp.float32) + bias.astype(jnp.float32)[:, None, None, None]
        for tap_pair in range(9):
            rad_off, azi_off = divmod(tap_pair, 3)
            w_block = weight_f[:, tap_pair * 3 * channels:(tap_pair + 1) * 3 * channels]
            stacked = stack_taps(padded, rad_off, azi_off, False)
            preact = preact + jnp.einsum("om,mrta->orta", w_block, stacked, precision=high)
        gate_value = jax.nn.sigmoid(preact)
        result = (preact * gate_value).astype(jnp.bfloat16)
        delta_z = (sample_grad.astype(jnp.float32) * gate_value * (1.0 + preact * (1.0 - gate_value))).astype(jnp.bfloat16)
        delta_pad = pad_field(delta_z)
        delta_f = delta_z.astype(jnp.float32)
        backward = jnp.zeros(sample_in.shape, jnp.float32)
        pieces = []
        for tap_pair in range(9):
            rad_off, azi_off = divmod(tap_pair, 3)
            w_block = weight_f[:, tap_pair * 3 * channels:(tap_pair + 1) * 3 * channels]
            w_back = w_block.reshape(out_rows, 3, channels).transpose(1, 0, 2).reshape(3 * out_rows, channels)
            dstack = stack_taps(delta_pad, 2 - rad_off, 2 - azi_off, True)
            backward = backward + jnp.einsum("mc,mrta->crta", w_back, dstack, precision=high)
            stacked = stack_taps(padded, rad_off, azi_off, False)
            pieces.append(jnp.einsum("orta,mrta->om", delta_f, stacked, precision=high))
        weight_term = jnp.concatenate(pieces, axis=1)
        bias_term = jnp.sum(delta_f, axis=(1, 2, 3))
        return result, backward.astype(jnp.bfloat16), weight_term, bias_term

    output, input_grad, weight_parts, bias_parts = lax.map(per_sample, (inputs, cotangent))
    weight_grad = jnp.sum(weight_parts, axis=0) * inverse_scale
    bias_grad = jnp.sum(bias_parts, axis=0) * inverse_scale
    return output, input_grad, weight_grad, bias_grad
```

```python
import functools

import jax
import jax.numpy as jnp
from jax import lax
from jax.experimental import pallas as pl
from jax.experimental.pallas import tpu as pltpu
from jax.sharding import PartitionSpec as P

inverse_scale = 1.0 / 1024.0
VMEM_LIMIT = 56 * 1024 * 1024


def stack_axial(value):
    extent = value.shape[1]
    lane = lax.broadcasted_iota(jnp.int32, value.shape, 1)
    wide = value.astype(jnp.float32)
    before = jnp.where(lane == 0, 0.0, pltpu.roll(wide, 1, 1)).astype(jnp.bfloat16)
    after = jnp.where(lane == extent - 1, 0.0, pltpu.roll(wide, extent - 1, 1)).astype(jnp.bfloat16)
    return jnp.concatenate([before, value, after], axis=0)


def columns(stacked, r, a):
    rows = []
    for i in range(3):
        for j in range(3):
            rows.append(stacked[r + i, a + j])
    return jnp.concatenate(rows, axis=0)


def fill(stacked, field, azi_lo, azi_hi, rad_lo, rad_hi):
    radial, azimuth = field.shape[0], field.shape[1]

    @pl.loop(0, radial * azimuth)
    def _(n):
        r, a = n // azimuth, n % azimuth
        stacked[r + 1, a + 1] = stack_axial(field[r, a])

    @pl.loop(0, radial)
    def _(r):
        stacked[r + 1, 0] = stack_axial(azi_lo[r])
        stacked[r + 1, azimuth + 1] = stack_axial(azi_hi[r])

    @pl.loop(0, azimuth + 2)
    def _(a):
        stacked[0, a] = stack_axial(rad_lo[a])
        stacked[radial + 1, a] = stack_axial(rad_hi[a])


def forward_kernel(
    field, azi_lo, azi_hi, rad_lo, rad_hi, weight, bias, cotangent,
    output, delta, weight_term, bias_term, stacked, turned, result, total, bias_total,
):
    radial, azimuth = field.shape[0], field.shape[1]
    fill(stacked, field, azi_lo, azi_hi, rad_lo, rad_hi)
    total[...] = jnp.zeros_like(total)
    bias_total[...] = jnp.zeros_like(bias_total)

    @pl.loop(0, radial)
    def _(r):
        turned[...] = jnp.swapaxes(cotangent[:, r], 0, 1)

        @pl.loop(0, azimuth)
        def _(a):
            col = columns(stacked, r, a)
            preact = jnp.dot(weight[...], col, preferred_element_type=jnp.float32)
            preact = preact + bias[...]
            gate = jax.nn.sigmoid(preact)
            result[a] = (preact * gate).astype(jnp.bfloat16)
            d = turned[a].astype(jnp.float32) * gate * (1.0 + preact * (1.0 - gate))
            d = d.astype(jnp.bfloat16)
            delta[r, a] = d
            bias_total[...] += d.astype(jnp.float32)
            total[...] += lax.dot_general(
                d, col, (((1,), (1,)), ((), ())), preferred_element_type=jnp.float32
            )

        output[:, r] = jnp.swapaxes(result[...], 0, 1)

    weight_term[...] = (total[...] * inverse_scale).astype(jnp.bfloat16)
    bias_term[...] = jnp.sum(bias_total[...], axis=1, keepdims=True) * inverse_scale


def backward_kernel(field, azi_lo, azi_hi, rad_lo, rad_hi, weight, output, stacked, result):
    radial, azimuth = field.shape[0], field.shape[1]
    fill(stacked, field, azi_lo, azi_hi, rad_lo, rad_hi)

    @pl.loop(0, radial)
    def _(r):
        @pl.loop(0, azimuth)
        def _(a):
            col = columns(stacked, r, a)
            result[a] = jnp.dot(
                weight[...], col, preferred_element_type=jnp.float32
            ).astype(jnp.bfloat16)

        output[:, r] = jnp.swapaxes(result[...], 0, 1)


def halos(field):
    rad_count, azi_count = lax.axis_size("rad"), lax.axis_size("azi")
    rad_index = lax.axis_index("rad")
    up = [(i, (i + 1) % azi_count) for i in range(azi_count)]
    down = [((i + 1) % azi_count, i) for i in range(azi_count)]
    azi_lo = lax.ppermute(field[:, -1], "azi", up)
    azi_hi = lax.ppermute(field[:, 0], "azi", down)

    def row(r):
        return jnp.concatenate([azi_lo[r][None], field[r], azi_hi[r][None]], axis=0)

    rad_lo = lax.ppermute(row(-1), "rad", [(i, i + 1) for i in range(rad_count - 1)])
    rad_hi = lax.ppermute(row(0), "rad", [(i + 1, i) for i in range(rad_count - 1)])
    return azi_lo, azi_hi, rad_lo, rad_hi


def on_device(inputs, weight, bias, cotangent):
    _, channels, radial, azimuth, axial = inputs.shape
    full_weight = lax.all_gather(weight, "dp", axis=0, tiled=True)
    full_bias = lax.all_gather(bias, "dp", axis=0, tiled=True)
    rows, depth = full_weight.shape
    taps = depth // channels
    back_weight = (
        full_weight.reshape(rows, taps, channels)[:, ::-1].transpose(2, 1, 0).reshape(channels, taps * rows)
    )
    field = inputs[0].transpose(1, 2, 0, 3)
    vmem = pl.BlockSpec(memory_space=pltpu.VMEM)
    shape = jax.ShapeDtypeStruct
    flops = 2 * rows * depth * radial * azimuth * axial
    output, delta, weight_term, bias_term = pl.pallas_call(
        forward_kernel,
        out_shape=(
            shape((rows, radial, azimuth, axial), jnp.bfloat16),
            shape((radial, azimuth, rows, axial), jnp.bfloat16),
            shape((rows, depth), jnp.bfloat16),
            shape((rows, 1), jnp.float32),
        ),
        in_specs=[vmem] * 8,
        out_specs=(vmem,) * 4,
        scratch_shapes=[
            pltpu.VMEM((radial + 2, azimuth + 2, 3 * channels, axial), jnp.bfloat16),
            pltpu.VMEM((azimuth, rows, axial), jnp.bfloat16),
            pltpu.VMEM((azimuth, rows, axial), jnp.bfloat16),
            pltpu.VMEM((rows, depth), jnp.float32),
            pltpu.VMEM((rows, axial), jnp.float32),
        ],
        compiler_params=pltpu.CompilerParams(vmem_limit_bytes=VMEM_LIMIT),
        cost_estimate=pl.CostEstimate(flops=2 * flops, bytes_accessed=8 << 20, transcendentals=0),
    )(field, *halos(field), full_weight, full_bias.astype(jnp.float32)[:, None], cotangent[0])
    input_grad = pl.pallas_call(
        backward_kernel,
        out_shape=shape((channels, radial, azimuth, axial), jnp.bfloat16),
        in_specs=[vmem] * 6,
        out_specs=vmem,
        scratch_shapes=[
            pltpu.VMEM((radial + 2, azimuth + 2, 3 * rows, axial), jnp.bfloat16),
            pltpu.VMEM((azimuth, channels, axial), jnp.bfloat16),
        ],
        compiler_params=pltpu.CompilerParams(vmem_limit_bytes=VMEM_LIMIT),
        cost_estimate=pl.CostEstimate(flops=flops, bytes_accessed=6 << 20, transcendentals=0),
    )(delta, *halos(delta), back_weight)
    weight_grad = lax.psum(
        lax.psum_scatter(weight_term, "dp", scatter_dimension=0, tiled=True).astype(jnp.float32),
        ("rad", "azi"),
    )
    bias_grad = lax.psum(
        lax.psum_scatter(bias_term[:, 0], "dp", scatter_dimension=0, tiled=True), ("rad", "azi")
    )
    return output[None], input_grad[None], weight_grad, bias_grad


def solution(mesh):
    field_spec = P("dp", None, "rad", "azi", None)
    return jax.shard_map(
        on_device,
        mesh=mesh,
        in_specs=(field_spec, P("dp", None), P("dp"), field_spec),
        out_specs=(field_spec, field_spec, P("dp", None), P("dp")),
        check_vma=False,
    )
```

```python
import functools

import jax
import jax.numpy as jnp
from jax import lax
from jax.experimental import pallas as pl
from jax.experimental.pallas import tpu as pltpu
from jax.sharding import PartitionSpec as P

inverse_scale = 1.0 / 1024.0
VMEM_LIMIT = 60 * 1024 * 1024
LANES = 128
MESH = pl.DeviceIdType.MESH
F32, BF16 = jnp.float32, jnp.bfloat16


def stack_axial(value):
    extent = value.shape[1]
    lane = lax.broadcasted_iota(jnp.int32, value.shape, 1)
    wide = value.astype(F32)
    before = jnp.where(lane == 0, 0.0, pltpu.roll(wide, 1, 1)).astype(BF16)
    after = jnp.where(lane == extent - 1, 0.0, pltpu.roll(wide, extent - 1, 1)).astype(BF16)
    return jnp.concatenate([before, value.astype(BF16), after], axis=0)


def pair_weights(full):
    width = full.shape[1] // 3
    zeros = jnp.zeros((full.shape[0], width // 3), full.dtype)
    low, high = [], []
    for i in range(3):
        part = full[:, i * width:(i + 1) * width]
        low += [part, zeros]
        high += [zeros, part]
    return jnp.concatenate(
        [jnp.concatenate(low, axis=1), jnp.concatenate(high, axis=1)], axis=0
    ).astype(BF16)


def pair_columns(stacked, r, a):
    return jnp.concatenate([stacked[r + i, a + j] for i in range(3) for j in range(4)], axis=0)


class Halo:
    def __init__(self, cells, send, recv):
        self.cells, self.send, self.recv = cells, send, recv
        self.radial, self.azimuth = cells.shape[0] - 2, cells.shape[1] - 2
        self.rad, self.rads = lax.axis_index("rad"), lax.axis_size("rad")
        azi, azis = lax.axis_index("azi"), lax.axis_size("azi")
        self.next, self.prev = lax.rem(azi + 1, azis), lax.rem(azi + azis - 1, azis)

    def copy(self, slot, source, target, where):
        return pltpu.make_async_remote_copy(
            src_ref=source, dst_ref=target, send_sem=self.send.at[slot],
            recv_sem=self.recv.at[slot], device_id=where, device_id_type=MESH,
        )

    def azi_copies(self, first, rows):
        cells, last = self.cells, self.azimuth
        return [
            self.copy(first, cells.at[rows, last], cells.at[rows, 0], {"azi": self.next}),
            self.copy(first + 1, cells.at[rows, 1], cells.at[rows, last + 1], {"azi": self.prev}),
        ]

    def main(self):
        return self.azi_copies(0, pl.ds(1, self.radial))

    def up(self):
        span = pl.ds(1, self.azimuth)
        return self.copy(2, self.cells.at[self.radial, span], self.cells.at[0, span], {"rad": self.rad + 1})

    def down(self):
        span = pl.ds(1, self.azimuth)
        return self.copy(
            3, self.cells.at[1, span], self.cells.at[self.radial + 1, span], {"rad": self.rad - 1}
        )

    def start(self):
        @pl.when(self.rad < self.rads - 1)
        def _():
            self.up().start()

        @pl.when(self.rad > 0)
        def _():
            self.down().start()

        for copy in self.main():
            copy.start()

    def wait_main(self):
        for copy in self.main():
            copy.wait()

    def finish_rim(self):
        @pl.when(self.rad > 0)
        def _():
            self.up().wait_recv()
            for copy in self.azi_copies(4, 0):
                copy.start()

        @pl.when(self.rad < self.rads - 1)
        def _():
            self.down().wait_recv()
            for copy in self.azi_copies(6, self.radial + 1):
                copy.start()

        @pl.when(self.rad == 0)
        def _():
            self.cells[0] = jnp.zeros(self.cells.shape[1:], BF16)

        @pl.when(self.rad == self.rads - 1)
        def _():
            self.cells[self.radial + 1] = jnp.zeros(self.cells.shape[1:], BF16)

        @pl.when(self.rad > 0)
        def _():
            self.down().wait_send()
            for copy in self.azi_copies(4, 0):
                copy.wait()

        @pl.when(self.rad < self.rads - 1)
        def _():
            self.up().wait_send()
            for copy in self.azi_copies(6, self.radial + 1):
                copy.wait()


def stack_rows(stacked, cells, first, count):
    @pl.loop(0, count)
    def _(a):
        stacked[first, a] = stack_axial(cells[first, a])


def kernel(
    field, mine, cotangent,
    output, input_grad, weight_grad, bias_grad,
    cells, dcells, stacked, dstacked, turned, result, dturned, total, bias_total,
    slots, pair_fwd, pair_back, bias_pair, part_out, part_in, piece_out, piece_in, final,
    halo_send, halo_recv, dhalo_send, dhalo_recv, w_send, w_recv, p_send, p_recv, q_send, q_recv, f_send, f_recv,
):
    channels, radial, azimuth, axial = field.shape
    dp, dps = lax.axis_index("dp"), lax.axis_size("dp")
    rad, azi, azis = lax.axis_index("rad"), lax.axis_index("azi"), lax.axis_size("azi")
    peers = lax.axis_size("rad") * azis
    me = rad * azis + azi
    rows = mine.shape[0]
    outs = rows * dps
    depth = mine.shape[1] - LANES
    block = depth // 27
    width = final.shape[2]

    def group(k):
        return lax.rem(dp + k, dps)

    def peer(k):
        other = lax.rem(me + k, peers)
        return {"rad": other // azis, "azi": lax.rem(other, azis)}

    barrier = pltpu.get_barrier_semaphore()

    @pl.loop(1, dps)
    def _(k):
        pl.semaphore_signal(barrier, inc=1, device_id={"dp": group(k)}, device_id_type=MESH)

    @pl.loop(1, peers)
    def _(k):
        pl.semaphore_signal(barrier, inc=1, device_id=peer(k), device_id_type=MESH)

    @pl.loop(0, radial)
    def _(r):
        cells[r + 1, pl.ds(1, azimuth)] = jnp.swapaxes(field[:, r], 0, 1)

    pl.semaphore_wait(barrier, dps + peers - 2)

    def w_copy(k):
        return pltpu.make_async_remote_copy(
            src_ref=mine, dst_ref=slots.at[dp], send_sem=w_send.at[k], recv_sem=w_recv.at[k],
            device_id={"dp": group(k)}, device_id_type=MESH,
        )

    halo = Halo(cells, halo_send, halo_recv)

    @pl.loop(1, dps)
    def _(k):
        w_copy(k).start()

    halo.start()
    slots[dp] = mine[...]
    total[...] = jnp.zeros_like(total)
    bias_total[...] = jnp.zeros_like(bias_total)

    @pl.loop(0, radial)
    def _(r):
        @pl.loop(1, azimuth + 1)
        def _(a):
            stacked[r + 1, a] = stack_axial(cells[r + 1, a])

    halo.wait_main()

    @pl.loop(0, radial)
    def _(r):
        for a in (0, azimuth + 1):
            stacked[r + 1, a] = stack_axial(cells[r + 1, a])

    @pl.loop(1, dps)
    def _(k):
        w_copy(k).wait()

    gathered = jnp.concatenate([slots[g].astype(F32) for g in range(dps)], axis=0)
    bias_pair[...] = jnp.concatenate([gathered[:, :LANES]] * 2, axis=0)
    full = gathered[:, LANES:]
    pair_fwd[...] = pair_weights(full)
    turned_weight = jnp.concatenate(
        [full[:, t * block:(t + 1) * block] for t in reversed(range(27))], axis=0
    ).T
    pair_back[...] = pair_weights(turned_weight)

    @pl.loop(0, radial)
    def _(n):
        r = lax.rem(n + 1, radial)

        @pl.when(n == radial - 2)
        def _():
            halo.finish_rim()
            stack_rows(stacked, cells, 0, azimuth + 2)
            stack_rows(stacked, cells, radial + 1, azimuth + 2)

        turned[...] = jnp.swapaxes(cotangent[:, r], 0, 1)

        @pl.loop(0, azimuth // 2)
        def _(pair):
            a = 2 * pair
            both = jnp.dot(pair_fwd[...], pair_columns(stacked, r, a), preferred_element_type=F32)
            both = both + bias_pair[:, :1]
            for p in range(2):
                preact = both[p * outs:(p + 1) * outs]
                gate = jax.nn.sigmoid(preact)
                result[a + p] = (preact * gate).astype(BF16)
                d = turned[a + p].astype(F32) * gate * (1.0 + preact * (1.0 - gate))
                d16 = d.astype(BF16)
                d = d16.astype(F32)
                dcells[r + 1, a + p + 1] = d16
                bias_total[...] += d
                dstacked[r + 1, a + p + 1] = stack_axial(d)
                pad = jnp.zeros((LANES - outs, axial), F32)
                dturned[a + p, pl.ds(pl.multiple_of(r * axial, axial), axial)] = (
                    jnp.concatenate([d, pad], axis=0).T.astype(BF16)
                )

        output[:, r] = jnp.swapaxes(result[...], 0, 1)

    dhalo = Halo(dcells, dhalo_send, dhalo_recv)
    dhalo.start()

    @pl.loop(0, azimuth // 2)
    def _(pair):
        a = 2 * pair
        right = jnp.concatenate([dturned[a], dturned[a + 1]], axis=1)
        for i in range(3):
            for j in range(4):
                left = jnp.concatenate([stacked[r + i, a + j] for r in range(radial)], axis=1)
                total[i, j] += jnp.dot(left, right, preferred_element_type=F32)

    dhalo.wait_main()
    dhalo.finish_rim()

    taps = [total[i, j, :, :LANES] + total[i, j + 1, :, LANES:] for i in range(3) for j in range(3)]
    grads = jnp.concatenate(taps, axis=0).T[:outs] * inverse_scale
    bias_sum = jnp.sum(bias_total[...], axis=1, keepdims=True) * inverse_scale
    fill = -(-depth // LANES) * LANES
    spare = peers * width - fill - LANES
    grads = jnp.concatenate(
        [grads, jnp.zeros((outs, fill - depth), F32), jnp.broadcast_to(bias_sum, (outs, LANES))]
        + ([jnp.zeros((outs, spare), F32)] if spare else []),
        axis=1,
    )
    for g in range(dps):
        for p in range(peers):
            part_out[g, p] = grads[g * rows:(g + 1) * rows, p * width:(p + 1) * width].astype(BF16)

    def p_copy(k):
        return pltpu.make_async_remote_copy(
            src_ref=part_out.at[group(k)], dst_ref=part_in.at[k], send_sem=p_send.at[k],
            recv_sem=p_recv.at[k], device_id={"dp": group(k)}, device_id_type=MESH,
        )

    def q_copy(k):
        return pltpu.make_async_remote_copy(
            src_ref=piece_out.at[lax.rem(me + k, peers)], dst_ref=piece_in.at[k], send_sem=q_send.at[k],
            recv_sem=q_recv.at[k], device_id=peer(k), device_id_type=MESH,
        )

    def f_copy(k):
        return pltpu.make_async_remote_copy(
            src_ref=final.at[me], dst_ref=final.at[me], send_sem=f_send.at[k],
            recv_sem=f_recv.at[k], device_id=peer(k), device_id_type=MESH,
        )

    @pl.loop(1, dps)
    def _(k):
        p_copy(k).start()

    @pl.loop(0, radial)
    def _(r):
        for a in (0, azimuth + 1):
            dstacked[r + 1, a] = stack_axial(dcells[r + 1, a])

    stack_rows(dstacked, dcells, 0, azimuth + 2)
    stack_rows(dstacked, dcells, radial + 1, azimuth + 2)

    @pl.loop(0, radial)
    def _(r):
        @pl.when(r == 1)
        def _():
            @pl.loop(1, dps)
            def _(k):
                p_copy(k).wait()

            @pl.loop(0, peers)
            def _(p):
                term = part_out[dp, p].astype(F32)
                for k in range(1, dps):
                    term = term + part_in[k, p].astype(F32)
                piece_out[p] = term.astype(BF16)

            @pl.loop(1, peers)
            def _(k):
                q_copy(k).start()

        @pl.when(r == radial - 1)
        def _():
            @pl.loop(1, peers)
            def _(k):
                q_copy(k).wait()

            term = piece_out[me].astype(F32)
            for k in range(1, peers):
                term = term + piece_in[k].astype(F32)
            final[me] = term.astype(BF16)

            @pl.loop(1, peers)
            def _(k):
                f_copy(k).start()

        @pl.loop(0, azimuth // 2)
        def _(pair):
            a = 2 * pair
            both = jnp.dot(pair_back[...], pair_columns(dstacked, r, a), preferred_element_type=F32)
            result[a] = both[:channels].astype(BF16)
            result[a + 1] = both[channels:].astype(BF16)

        input_grad[:, r] = jnp.swapaxes(result[...], 0, 1)

    @pl.loop(1, peers)
    def _(k):
        f_copy(k).wait()

    for p in range(peers):
        stop = min(depth, (p + 1) * width)
        if stop > p * width:
            weight_grad[:, p * width:stop] = final[p].astype(F32)[:, :stop - p * width]
        if p * width <= fill < (p + 1) * width:
            bias_grad[...] = final[p, :, fill - p * width:fill - p * width + LANES].astype(F32)


def on_device(inputs, weight, bias, cotangent):
    _, channels, radial, azimuth, axial = inputs.shape
    rows, depth = weight.shape
    dps, peers = lax.axis_size("dp"), lax.axis_size("rad") * lax.axis_size("azi")
    outs = rows * dps
    tiles = -(-depth // LANES) + 1
    width = -(-tiles // peers) * LANES
    mine = jnp.concatenate([jnp.broadcast_to(bias[:, None], (rows, LANES)), weight], axis=1)
    vmem = pl.BlockSpec(memory_space=pltpu.VMEM)
    shape = jax.ShapeDtypeStruct
    dma = pltpu.SemaphoreType.DMA
    output, input_grad, weight_grad, bias_grad = pl.pallas_call(
        kernel,
        out_shape=(
            shape((outs, radial, azimuth, axial), BF16),
            shape((channels, radial, azimuth, axial), BF16),
            shape((rows, depth), F32),
            shape((rows, LANES), F32),
        ),
        in_specs=[vmem] * 3,
        out_specs=(vmem,) * 4,
        scratch_shapes=[
            pltpu.VMEM((radial + 2, azimuth + 2, channels, axial), BF16),
            pltpu.VMEM((radial + 2, azimuth + 2, outs, axial), BF16),
            pltpu.VMEM((radial + 2, azimuth + 2, 3 * channels, axial), BF16),
            pltpu.VMEM((radial + 2, azimuth + 2, 3 * outs, axial), BF16),
            pltpu.VMEM((azimuth, outs, axial), BF16),
            pltpu.VMEM((azimuth, outs, axial), BF16),
            pltpu.VMEM((azimuth, radial * axial, LANES), BF16),
            pltpu.VMEM((3, 4, 3 * channels, 2 * LANES), F32),
            pltpu.VMEM((outs, axial), F32),
            pltpu.VMEM((dps, rows, depth + LANES), BF16),
            pltpu.VMEM((2 * outs, 4 * depth // 3), BF16),
            pltpu.VMEM((2 * channels, 36 * outs), BF16),
            pltpu.VMEM((2 * outs, LANES), F32),
            pltpu.VMEM((dps, peers, rows, width), BF16),
            pltpu.VMEM((dps, peers, rows, width), BF16),
            pltpu.VMEM((peers, rows, width), BF16),
            pltpu.VMEM((peers, rows, width), BF16),
            pltpu.VMEM((peers, rows, width), BF16),
            dma((8,)), dma((8,)), dma((8,)), dma((8,)),
            dma((dps,)), dma((dps,)), dma((dps,)), dma((dps,)),
            dma((peers,)), dma((peers,)), dma((peers,)), dma((peers,)),
        ],
        compiler_params=pltpu.CompilerParams(
            vmem_limit_bytes=VMEM_LIMIT, collective_id=0, has_side_effects=True
        ),
    )(inputs[0], mine, cotangent[0])
    return output[None], input_grad[None], weight_grad, bias_grad[:, 0]


def solution(mesh):
    field_spec = P("dp", None, "rad", "azi", None)
    return jax.shard_map(
        on_device,
        mesh=mesh,
        in_specs=(field_spec, P("dp", None), P("dp"), field_spec),
        out_specs=(field_spec, field_spec, P("dp", None), P("dp")),
        check_vma=False,
    )
```

```python
import functools

import jax
import jax.numpy as jnp
from jax import lax
from jax.experimental import pallas as pl
from jax.experimental.pallas import tpu as pltpu
from jax.sharding import PartitionSpec as P

inverse_scale = 1.0 / 1024.0
VMEM_LIMIT = 60 * 1024 * 1024
LANES = 128
MESH = pl.DeviceIdType.MESH
F32, BF16 = jnp.float32, jnp.bfloat16


def shift(value, step, axis):
    extent = value.shape[axis]
    place = lax.broadcasted_iota(jnp.int32, value.shape, axis)
    edge = 0 if step == 1 else extent - 1
    return jnp.where(place == edge, 0.0, pltpu.roll(value, step % extent, axis))


def columns(cells, r, a):
    return jnp.concatenate([cells[r + i, a + j] for i in range(3) for j in range(3)], axis=0)


def convolve(weight, cells, r, a):
    stacked = jnp.dot(weight, columns(cells, r, a), preferred_element_type=F32)
    rows = stacked.shape[0] // 3
    return (
        stacked[rows:2 * rows]
        + shift(stacked[:rows], 1, 1)
        + shift(stacked[2 * rows:], -1, 1)
    )


class Halo:
    def __init__(self, cells, send, recv):
        self.cells, self.send, self.recv = cells, send, recv
        self.radial, self.azimuth = cells.shape[0] - 2, cells.shape[1] - 2
        self.rad, self.rads = lax.axis_index("rad"), lax.axis_size("rad")
        azi, azis = lax.axis_index("azi"), lax.axis_size("azi")
        self.next, self.prev = lax.rem(azi + 1, azis), lax.rem(azi + azis - 1, azis)

    def copy(self, slot, source, target, where):
        return pltpu.make_async_remote_copy(
            src_ref=source, dst_ref=target, send_sem=self.send.at[slot],
            recv_sem=self.recv.at[slot], device_id=where, device_id_type=MESH,
        )

    def azi_copies(self, first, rows):
        cells, last = self.cells, self.azimuth
        return [
            self.copy(first, cells.at[rows, last], cells.at[rows, 0], {"azi": self.next}),
            self.copy(first + 1, cells.at[rows, 1], cells.at[rows, last + 1], {"azi": self.prev}),
        ]

    def main(self):
        return self.azi_copies(0, pl.ds(1, self.radial))

    def up(self):
        span = pl.ds(1, self.azimuth)
        return self.copy(2, self.cells.at[self.radial, span], self.cells.at[0, span], {"rad": self.rad + 1})

    def down(self):
        span = pl.ds(1, self.azimuth)
        return self.copy(
            3, self.cells.at[1, span], self.cells.at[self.radial + 1, span], {"rad": self.rad - 1}
        )

    def start(self):
        @pl.when(self.rad < self.rads - 1)
        def _():
            self.up().start()

        @pl.when(self.rad > 0)
        def _():
            self.down().start()

        for copy in self.main():
            copy.start()

    def wait_main(self):
        for copy in self.main():
            copy.wait()

    def finish_rim(self):
        @pl.when(self.rad > 0)
        def _():
            self.up().wait_recv()
            for copy in self.azi_copies(4, 0):
                copy.start()

        @pl.when(self.rad < self.rads - 1)
        def _():
            self.down().wait_recv()
            for copy in self.azi_copies(6, self.radial + 1):
                copy.start()

        @pl.when(self.rad == 0)
        def _():
            self.cells[0] = jnp.zeros(self.cells.shape[1:], BF16)

        @pl.when(self.rad == self.rads - 1)
        def _():
            self.cells[self.radial + 1] = jnp.zeros(self.cells.shape[1:], BF16)

        @pl.when(self.rad > 0)
        def _():
            self.down().wait_send()
            for copy in self.azi_copies(4, 0):
                copy.wait()

        @pl.when(self.rad < self.rads - 1)
        def _():
            self.up().wait_send()
            for copy in self.azi_copies(6, self.radial + 1):
                copy.wait()


def kernel(
    field, weight, bias, cotangent,
    output, input_grad, weight_grad, bias_grad,
    cells, dcells, turned, result, dturned, total, bias_total,
    mine, slots, fwd_weight, back_weight, bias_column, part_out, part_in, piece_out, piece_in, final,
    halo_send, halo_recv, dhalo_send, dhalo_recv, w_send, w_recv, p_send, p_recv, q_send, q_recv, f_send, f_recv,
):
    channels, radial, azimuth, axial = field.shape
    dp, dps = lax.axis_index("dp"), lax.axis_size("dp")
    rad, azi, azis = lax.axis_index("rad"), lax.axis_index("azi"), lax.axis_size("azi")
    peers = lax.axis_size("rad") * azis
    me = rad * azis + azi
    rows, depth = weight.shape
    outs = rows * dps
    block = depth // 27
    width = final.shape[2]
    span = (mine.shape[1] - LANES) // 3

    def group(k):
        return lax.rem(dp + k, dps)

    def peer(k):
        other = lax.rem(me + k, peers)
        return {"rad": other // azis, "azi": lax.rem(other, azis)}

    barrier = pltpu.get_barrier_semaphore()

    @pl.loop(1, dps)
    def _(k):
        pl.semaphore_signal(barrier, inc=1, device_id={"dp": group(k)}, device_id_type=MESH)

    @pl.loop(1, peers)
    def _(k):
        pl.semaphore_signal(barrier, inc=1, device_id=peer(k), device_id_type=MESH)

    own = weight[...].astype(F32)
    pad = jnp.zeros((rows, span - 9 * block), F32)
    for k in range(3):
        parts = [own[:, t * block:(t + 1) * block] for t in range(k, 27, 3)]
        mine[:, LANES + k * span:LANES + (k + 1) * span] = jnp.concatenate(parts + [pad], axis=1).astype(BF16)
    row = lax.broadcasted_iota(jnp.int32, (rows, rows), 0)
    col = lax.broadcasted_iota(jnp.int32, (rows, rows), 1)
    column = jnp.sum(jnp.where(row == col, bias[...].astype(F32), 0.0), axis=1, keepdims=True)
    mine[:, :LANES] = jnp.broadcast_to(column, (rows, LANES)).astype(BF16)

    @pl.loop(0, radial)
    def _(r):
        cells[r + 1, pl.ds(1, azimuth)] = jnp.swapaxes(field[:, r], 0, 1)

    pl.semaphore_wait(barrier, dps + peers - 2)

    def w_copy(k):
        return pltpu.make_async_remote_copy(
            src_ref=mine, dst_ref=slots.at[dp], send_sem=w_send.at[k], recv_sem=w_recv.at[k],
            device_id={"dp": group(k)}, device_id_type=MESH,
        )

    halo = Halo(cells, halo_send, halo_recv)

    @pl.loop(1, dps)
    def _(k):
        w_copy(k).start()

    halo.start()
    slots[dp] = mine[...]
    total[...] = jnp.zeros_like(total)
    bias_total[...] = jnp.zeros_like(bias_total)
    halo.wait_main()

    @pl.loop(1, dps)
    def _(k):
        w_copy(k).wait()

    gathered = jnp.concatenate([slots[g].astype(F32) for g in range(dps)], axis=0)
    bias_column[...] = gathered[:, :LANES]
    for k in range(3):
        start = LANES + k * span
        part = gathered[:, start:start + 9 * block]
        fwd_weight[k * outs:(k + 1) * outs] = part.astype(BF16)
        flipped = [part[:, t * block:(t + 1) * block] for t in reversed(range(9))]
        back_weight[(2 - k) * channels:(3 - k) * channels] = (
            jnp.concatenate(flipped, axis=0).T.astype(BF16)
        )

    @pl.loop(0, radial)
    def _(n):
        r = lax.rem(n + 1, radial)

        @pl.when(n == radial - 2)
        def _():
            halo.finish_rim()

        turned[...] = jnp.swapaxes(cotangent[:, r], 0, 1)

        @pl.loop(0, azimuth // 2)
        def _(pair):
            for p in range(2):
                a = 2 * pair + p
                preact = convolve(fwd_weight[...], cells, r, a) + bias_column[:, :1]
                gate = 0.5 * jnp.tanh(0.5 * preact) + 0.5
                result[a] = (preact * gate).astype(BF16)
                d = turned[a].astype(F32) * gate * (1.0 + preact * (1.0 - gate))
                d16 = d.astype(BF16)
                d = d16.astype(F32)
                dcells[r + 1, a + 1] = d16
                bias_total[...] += d
                flat = jnp.concatenate([d, jnp.zeros((LANES - outs, axial), F32)], axis=0).T
                dturned[a, pl.ds(pl.multiple_of(r * axial, axial), axial)] = jnp.concatenate(
                    [shift(flat, -1, 0), flat, shift(flat, 1, 0)], axis=1
                ).astype(BF16)

        output[:, r] = jnp.swapaxes(result[...], 0, 1)

    dhalo = Halo(dcells, dhalo_send, dhalo_recv)
    dhalo.start()

    @pl.loop(0, azimuth)
    def _(a):
        right = dturned[a]
        for i in range(3):
            left = jnp.concatenate(
                [jnp.concatenate([cells[r + i, a + j] for j in range(3)], axis=0) for r in range(radial)],
                axis=1,
            )
            total[i] += jnp.dot(left, right, preferred_element_type=F32)

    dhalo.wait_main()
    dhalo.finish_rim()

    taps = [
        total[i, j * channels:(j + 1) * channels, k * LANES:(k + 1) * LANES]
        for i in range(3) for j in range(3) for k in range(3)
    ]
    grads = jnp.concatenate(taps, axis=0).T[:outs] * inverse_scale
    bias_sum = jnp.sum(bias_total[...], axis=1, keepdims=True) * inverse_scale
    fill = -(-depth // LANES) * LANES
    spare = peers * width - fill - LANES
    grads = jnp.concatenate(
        [grads, jnp.zeros((outs, fill - depth), F32), jnp.broadcast_to(bias_sum, (outs, LANES))]
        + ([jnp.zeros((outs, spare), F32)] if spare else []),
        axis=1,
    )
    for g in range(dps):
        for p in range(peers):
            part_out[g, p] = grads[g * rows:(g + 1) * rows, p * width:(p + 1) * width].astype(BF16)

    def p_copy(k):
        return pltpu.make_async_remote_copy(
            src_ref=part_out.at[group(k)], dst_ref=part_in.at[k], send_sem=p_send.at[k],
            recv_sem=p_recv.at[k], device_id={"dp": group(k)}, device_id_type=MESH,
        )

    def q_copy(k):
        return pltpu.make_async_remote_copy(
            src_ref=piece_out.at[lax.rem(me + k, peers)], dst_ref=piece_in.at[k], send_sem=q_send.at[k],
            recv_sem=q_recv.at[k], device_id=peer(k), device_id_type=MESH,
        )

    def f_copy(k):
        return pltpu.make_async_remote_copy(
            src_ref=final.at[me], dst_ref=final.at[me], send_sem=f_send.at[k],
            recv_sem=f_recv.at[k], device_id=peer(k), device_id_type=MESH,
        )

    @pl.loop(1, dps)
    def _(k):
        p_copy(k).start()

    @pl.loop(0, radial)
    def _(r):
        @pl.when(r == 1)
        def _():
            @pl.loop(1, dps)
            def _(k):
                p_copy(k).wait()

            @pl.loop(0, peers)
            def _(p):
                term = part_out[dp, p].astype(F32)
                for k in range(1, dps):
                    term = term + part_in[k, p].astype(F32)
                piece_out[p] = term.astype(BF16)

            @pl.loop(1, peers)
            def _(k):
                q_copy(k).start()

        @pl.when(r == radial - 1)
        def _():
            @pl.loop(1, peers)
            def _(k):
                q_copy(k).wait()

            term = piece_out[me].astype(F32)
            for k in range(1, peers):
                term = term + piece_in[k].astype(F32)
            final[me] = term.astype(BF16)

            @pl.loop(1, peers)
            def _(k):
                f_copy(k).start()

        @pl.loop(0, azimuth // 2)
        def _(pair):
            for p in range(2):
                a = 2 * pair + p
                result[a] = convolve(back_weight[...], dcells, r, a).astype(BF16)

        input_grad[:, r] = jnp.swapaxes(result[...], 0, 1)

    @pl.loop(1, peers)
    def _(k):
        f_copy(k).wait()

    for p in range(peers):
        stop = min(depth, (p + 1) * width)
        if stop > p * width:
            weight_grad[:, p * width:stop] = final[p].astype(F32)[:, :stop - p * width]
        if p * width <= fill < (p + 1) * width:
            column = final[p, :, fill - p * width:fill - p * width + LANES].astype(F32)[:, :1]
            bias_grad[...] = jnp.sum(jnp.where(row == col, column, 0.0), axis=0, keepdims=True)


def on_device(inputs, weight, bias, cotangent):
    _, channels, radial, azimuth, axial = inputs.shape
    rows, depth = weight.shape
    dps, peers = lax.axis_size("dp"), lax.axis_size("rad") * lax.axis_size("azi")
    outs = rows * dps
    tiles = -(-depth // LANES) + 1
    width = -(-tiles // peers) * LANES
    span = -(-depth // 3 // LANES) * LANES
    vmem = pl.BlockSpec(memory_space=pltpu.VMEM)
    shape = jax.ShapeDtypeStruct
    dma = pltpu.SemaphoreType.DMA
    output, input_grad, weight_grad, bias_grad = pl.pallas_call(
        kernel,
        out_shape=(
            shape((outs, radial, azimuth, axial), BF16),
            shape((channels, radial, azimuth, axial), BF16),
            shape((rows, depth), F32),
            shape((1, rows), F32),
        ),
        in_specs=[vmem] * 4,
        out_specs=(vmem,) * 4,
        scratch_shapes=[
            pltpu.VMEM((radial + 2, azimuth + 2, channels, axial), BF16),
            pltpu.VMEM((radial + 2, azimuth + 2, outs, axial), BF16),
            pltpu.VMEM((azimuth, outs, axial), BF16),
            pltpu.VMEM((azimuth, outs, axial), BF16),
            pltpu.VMEM((azimuth, radial * axial, 3 * LANES), BF16),
            pltpu.VMEM((3, 3 * channels, 3 * LANES), F32),
            pltpu.VMEM((outs, axial), F32),
            pltpu.VMEM((rows, LANES + 3 * span), BF16),
            pltpu.VMEM((dps, rows, LANES + 3 * span), BF16),
            pltpu.VMEM((3 * outs, 9 * channels), BF16),
            pltpu.VMEM((3 * channels, 9 * outs), BF16),
            pltpu.VMEM((outs, LANES), F32),
            pltpu.VMEM((dps, peers, rows, width), BF16),
            pltpu.VMEM((dps, peers, rows, width), BF16),
            pltpu.VMEM((peers, rows, width), BF16),
            pltpu.VMEM((peers, rows, width), BF16),
            pltpu.VMEM((peers, rows, width), BF16),
            dma((8,)), dma((8,)), dma((8,)), dma((8,)),
            dma((dps,)), dma((dps,)), dma((dps,)), dma((dps,)),
            dma((peers,)), dma((peers,)), dma((peers,)), dma((peers,)),
        ],
        compiler_params=pltpu.CompilerParams(
            vmem_limit_bytes=VMEM_LIMIT, collective_id=0, has_side_effects=True
        ),
    )(inputs[0], weight, bias[None], cotangent[0])
    return output[None], input_grad[None], weight_grad, bias_grad[0]


def solution(mesh):
    field_spec = P("dp", None, "rad", "azi", None)
    return jax.shard_map(
        on_device,
        mesh=mesh,
        in_specs=(field_spec, P("dp", None), P("dp"), field_spec),
        out_specs=(field_spec, field_spec, P("dp", None), P("dp")),
        check_vma=False,
    )
```

```python
import functools

import jax
import jax.numpy as jnp
from jax import lax
from jax.experimental import pallas as pl
from jax.experimental.pallas import tpu as pltpu
from jax.sharding import PartitionSpec as P

inverse_scale = 1.0 / 1024.0
VMEM_LIMIT = 60 * 1024 * 1024
LANES = 128
MESH = pl.DeviceIdType.MESH
F32, BF16 = jnp.float32, jnp.bfloat16


def shift(value, step, axis):
    extent = value.shape[axis]
    place = lax.broadcasted_iota(jnp.int32, value.shape, axis)
    edge = 0 if step == 1 else extent - 1
    return jnp.where(place == edge, 0.0, pltpu.roll(value, step % extent, axis))


def columns(cells, r, a):
    return jnp.concatenate([cells[r + i, a + j] for i in range(3) for j in range(3)], axis=0)


def convolve(weight, cells, r, a):
    stacked = jnp.dot(weight, columns(cells, r, a), preferred_element_type=F32)
    rows = stacked.shape[0] // 3
    return (
        stacked[rows:2 * rows]
        + shift(stacked[:rows], 1, 1)
        + shift(stacked[2 * rows:], -1, 1)
    )


class Halo:
    def __init__(self, cells, send, recv):
        self.cells, self.send, self.recv = cells, send, recv
        self.radial, self.azimuth = cells.shape[0] - 2, cells.shape[1] - 2
        self.rad, self.rads = lax.axis_index("rad"), lax.axis_size("rad")
        azi, azis = lax.axis_index("azi"), lax.axis_size("azi")
        self.next, self.prev = lax.rem(azi + 1, azis), lax.rem(azi + azis - 1, azis)

    def copy(self, slot, source, target, where):
        return pltpu.make_async_remote_copy(
            src_ref=source, dst_ref=target, send_sem=self.send.at[slot],
            recv_sem=self.recv.at[slot], device_id=where, device_id_type=MESH,
        )

    def azi_copies(self, first, rows):
        cells, last = self.cells, self.azimuth
        return [
            self.copy(first, cells.at[rows, last], cells.at[rows, 0], {"azi": self.next}),
            self.copy(first + 1, cells.at[rows, 1], cells.at[rows, last + 1], {"azi": self.prev}),
        ]

    def main(self):
        return self.azi_copies(0, pl.ds(1, self.radial))

    def up(self):
        span = pl.ds(1, self.azimuth)
        return self.copy(2, self.cells.at[self.radial, span], self.cells.at[0, span], {"rad": self.rad + 1})

    def down(self):
        span = pl.ds(1, self.azimuth)
        return self.copy(
            3, self.cells.at[1, span], self.cells.at[self.radial + 1, span], {"rad": self.rad - 1}
        )

    def start(self):
        @pl.when(self.rad < self.rads - 1)
        def _():
            self.up().start()

        @pl.when(self.rad > 0)
        def _():
            self.down().start()

        for copy in self.main():
            copy.start()

    def wait_main(self):
        for copy in self.main():
            copy.wait()

    def finish_rim(self):
        @pl.when(self.rad > 0)
        def _():
            self.up().wait_recv()
            for copy in self.azi_copies(4, 0):
                copy.start()

        @pl.when(self.rad < self.rads - 1)
        def _():
            self.down().wait_recv()
            for copy in self.azi_copies(6, self.radial + 1):
                copy.start()

        @pl.when(self.rad == 0)
        def _():
            self.cells[0] = jnp.zeros(self.cells.shape[1:], BF16)

        @pl.when(self.rad == self.rads - 1)
        def _():
            self.cells[self.radial + 1] = jnp.zeros(self.cells.shape[1:], BF16)

        @pl.when(self.rad > 0)
        def _():
            self.down().wait_send()
            for copy in self.azi_copies(4, 0):
                copy.wait()

        @pl.when(self.rad < self.rads - 1)
        def _():
            self.up().wait_send()
            for copy in self.azi_copies(6, self.radial + 1):
                copy.wait()


def kernel(
    field, weight, bias, cotangent,
    output, input_grad, weight_grad, bias_grad,
    cells, dcells, given, turned, result, back_result, dturned, total, bias_total,
    mine, slots, fwd_weight, back_weight, bias_column, part_out, part_in, piece_out, piece_in, final,
    halo_send, halo_recv, dhalo_send, dhalo_recv, w_send, w_recv, p_send, p_recv, q_send, q_recv, f_send, f_recv,
    in_sem, out_sem, back_sem,
):
    channels, radial, azimuth, axial = field.shape
    dp, dps = lax.axis_index("dp"), lax.axis_size("dp")
    rad, azi, azis = lax.axis_index("rad"), lax.axis_index("azi"), lax.axis_size("azi")
    peers = lax.axis_size("rad") * azis
    me = rad * azis + azi
    rows, depth = weight.shape
    outs = rows * dps
    block = depth // 27
    width = final.shape[2]
    span = (mine.shape[1] - LANES) // 3

    def group(k):
        return lax.rem(dp + k, dps)

    def peer(k):
        other = lax.rem(me + k, peers)
        return {"rad": other // azis, "azi": lax.rem(other, azis)}

    def out_copy(r):
        return pltpu.make_async_copy(result.at[r], output.at[r], out_sem.at[r])

    def back_copy(r):
        return pltpu.make_async_copy(back_result.at[r], input_grad.at[r], back_sem.at[r])

    barrier = pltpu.get_barrier_semaphore()

    given_copy = pltpu.make_async_copy(cotangent, given, in_sem)
    given_copy.start()

    @pl.loop(1, dps)
    def _(k):
        pl.semaphore_signal(barrier, inc=1, device_id={"dp": group(k)}, device_id_type=MESH)

    @pl.loop(1, peers)
    def _(k):
        pl.semaphore_signal(barrier, inc=1, device_id=peer(k), device_id_type=MESH)

    own = weight[...].astype(F32)
    pad = jnp.zeros((rows, span - 9 * block), F32)
    for k in range(3):
        parts = [own[:, t * block:(t + 1) * block] for t in range(k, 27, 3)]
        mine[:, LANES + k * span:LANES + (k + 1) * span] = jnp.concatenate(parts + [pad], axis=1).astype(BF16)
    row = lax.broadcasted_iota(jnp.int32, (rows, rows), 0)
    col = lax.broadcasted_iota(jnp.int32, (rows, rows), 1)
    column = jnp.sum(jnp.where(row == col, bias[...].astype(F32), 0.0), axis=1, keepdims=True)
    mine[:, :LANES] = jnp.broadcast_to(column, (rows, LANES)).astype(BF16)

    @pl.loop(0, radial)
    def _(r):
        cells[r + 1, pl.ds(1, azimuth)] = jnp.swapaxes(field[:, r], 0, 1)

    pl.semaphore_wait(barrier, dps + peers - 2)

    def w_copy(k):
        return pltpu.make_async_remote_copy(
            src_ref=mine, dst_ref=slots.at[dp], send_sem=w_send.at[k], recv_sem=w_recv.at[k],
            device_id={"dp": group(k)}, device_id_type=MESH,
        )

    halo = Halo(cells, halo_send, halo_recv)

    @pl.loop(1, dps)
    def _(k):
        w_copy(k).start()

    halo.start()
    slots[dp] = mine[...]
    total[...] = jnp.zeros_like(total)
    bias_total[...] = jnp.zeros_like(bias_total)
    given_copy.wait()

    @pl.loop(0, radial)
    def _(r):
        turned[r] = jnp.swapaxes(given[:, r], 0, 1)

    halo.wait_main()

    @pl.loop(1, dps)
    def _(k):
        w_copy(k).wait()

    gathered = jnp.concatenate([slots[g].astype(F32) for g in range(dps)], axis=0)
    bias_column[...] = gathered[:, :LANES]
    for k in range(3):
        start = LANES + k * span
        part = gathered[:, start:start + 9 * block]
        fwd_weight[k * outs:(k + 1) * outs] = part.astype(BF16)
        flipped = [part[:, t * block:(t + 1) * block] for t in reversed(range(9))]
        back_weight[(2 - k) * channels:(3 - k) * channels] = (
            jnp.concatenate(flipped, axis=0).T.astype(BF16)
        )

    @pl.loop(0, radial)
    def _(n):
        r = lax.rem(n + 1, radial)

        @pl.when(n == radial - 2)
        def _():
            halo.finish_rim()

        @pl.loop(0, azimuth // 2)
        def _(pair):
            for p in range(2):
                a = 2 * pair + p
                preact = convolve(fwd_weight[...], cells, r, a) + bias_column[:, :1]
                gate = 0.5 * jnp.tanh(0.5 * preact) + 0.5
                result[r, a] = (preact * gate).astype(BF16)
                d = turned[r, a].astype(F32) * gate * (1.0 + preact * (1.0 - gate))
                d16 = d.astype(BF16)
                d = d16.astype(F32)
                dcells[r + 1, a + 1] = d16
                bias_total[...] += d
                flat = jnp.concatenate([d, jnp.zeros((LANES - outs, axial), F32)], axis=0).T
                dturned[a, pl.ds(pl.multiple_of(r * axial, axial), axial)] = jnp.concatenate(
                    [shift(flat, -1, 0), flat, shift(flat, 1, 0)], axis=1
                ).astype(BF16)

        out_copy(r).start()

    dhalo = Halo(dcells, dhalo_send, dhalo_recv)
    dhalo.start()

    @pl.loop(0, azimuth)
    def _(a):
        right = dturned[a]
        for i in range(3):
            left = jnp.concatenate(
                [jnp.concatenate([cells[r + i, a + j] for j in range(3)], axis=0) for r in range(radial)],
                axis=1,
            )
            total[i] += jnp.dot(left, right, preferred_element_type=F32)

    taps = [
        total[i, j * channels:(j + 1) * channels, k * LANES:(k + 1) * LANES]
        for i in range(3) for j in range(3) for k in range(3)
    ]
    grads = jnp.concatenate(taps, axis=0).T[:outs] * inverse_scale
    bias_sum = jnp.sum(bias_total[...], axis=1, keepdims=True) * inverse_scale
    fill = -(-depth // LANES) * LANES
    spare = peers * width - fill - LANES
    grads = jnp.concatenate(
        [grads, jnp.zeros((outs, fill - depth), F32), jnp.broadcast_to(bias_sum, (outs, LANES))]
        + ([jnp.zeros((outs, spare), F32)] if spare else []),
        axis=1,
    )
    for g in range(dps):
        for p in range(peers):
            part_out[g, p] = grads[g * rows:(g + 1) * rows, p * width:(p + 1) * width].astype(BF16)

    def p_copy(k):
        return pltpu.make_async_remote_copy(
            src_ref=part_out.at[group(k)], dst_ref=part_in.at[k], send_sem=p_send.at[k],
            recv_sem=p_recv.at[k], device_id={"dp": group(k)}, device_id_type=MESH,
        )

    def q_copy(k):
        return pltpu.make_async_remote_copy(
            src_ref=piece_out.at[lax.rem(me + k, peers)], dst_ref=piece_in.at[k], send_sem=q_send.at[k],
            recv_sem=q_recv.at[k], device_id=peer(k), device_id_type=MESH,
        )

    def f_copy(k):
        return pltpu.make_async_remote_copy(
            src_ref=final.at[me], dst_ref=final.at[me], send_sem=f_send.at[k],
            recv_sem=f_recv.at[k], device_id=peer(k), device_id_type=MESH,
        )

    @pl.loop(1, dps)
    def _(k):
        p_copy(k).start()

    dhalo.wait_main()
    pairs = azimuth // 2
    steps = radial * pairs

    @pl.loop(0, steps)
    def _(step):
        r = lax.rem(step // pairs + 1, radial)
        pair = lax.rem(step, pairs)

        @pl.when(step == (radial - 2) * pairs)
        def _():
            dhalo.finish_rim()

        @pl.when(step == steps // 2)
        def _():
            @pl.loop(1, dps)
            def _(k):
                p_copy(k).wait()

            @pl.loop(0, peers)
            def _(p):
                term = part_out[dp, p].astype(F32)
                for k in range(1, dps):
                    term = term + part_in[k, p].astype(F32)
                piece_out[p] = term.astype(BF16)

            @pl.loop(1, peers)
            def _(k):
                q_copy(k).start()

        @pl.when(step == 3 * steps // 4)
        def _():
            @pl.loop(1, peers)
            def _(k):
                q_copy(k).wait()

            term = piece_out[me].astype(F32)
            for k in range(1, peers):
                term = term + piece_in[k].astype(F32)
            final[me] = term.astype(BF16)

            @pl.loop(1, peers)
            def _(k):
                f_copy(k).start()

        for p in range(2):
            a = 2 * pair + p
            back_result[r, a] = convolve(back_weight[...], dcells, r, a).astype(BF16)

        @pl.when(pair == pairs - 1)
        def _():
            back_copy(r).start()

    @pl.loop(1, peers)
    def _(k):
        f_copy(k).wait()

    for p in range(peers):
        stop = min(depth, (p + 1) * width)
        if stop > p * width:
            weight_grad[:, p * width:stop] = final[p].astype(F32)[:, :stop - p * width]
        if p * width <= fill < (p + 1) * width:
            column = final[p, :, fill - p * width:fill - p * width + LANES].astype(F32)[:, :1]
            bias_grad[...] = jnp.sum(jnp.where(row == col, column, 0.0), axis=0, keepdims=True)

    @pl.loop(0, radial)
    def _(r):
        out_copy(r).wait()
        back_copy(r).wait()


def on_device(inputs, weight, bias, cotangent):
    _, channels, radial, azimuth, axial = inputs.shape
    rows, depth = weight.shape
    dps, peers = lax.axis_size("dp"), lax.axis_size("rad") * lax.axis_size("azi")
    outs = rows * dps
    tiles = -(-depth // LANES) + 1
    width = -(-tiles // peers) * LANES
    span = -(-depth // 3 // LANES) * LANES
    vmem = pl.BlockSpec(memory_space=pltpu.VMEM)
    anywhere = pl.BlockSpec(memory_space=pl.ANY)
    shape = jax.ShapeDtypeStruct
    dma = pltpu.SemaphoreType.DMA
    output, input_grad, weight_grad, bias_grad = pl.pallas_call(
        kernel,
        out_shape=(
            shape((radial, azimuth, outs, axial), BF16),
            shape((radial, azimuth, channels, axial), BF16),
            shape((rows, depth), F32),
            shape((1, rows), F32),
        ),
        in_specs=[vmem] * 3 + [anywhere],
        out_specs=(anywhere, anywhere, vmem, vmem),
        scratch_shapes=[
            pltpu.VMEM((radial + 2, azimuth + 2, channels, axial), BF16),
            pltpu.VMEM((radial + 2, azimuth + 2, outs, axial), BF16),
            pltpu.VMEM((outs, radial, azimuth, axial), BF16),
            pltpu.VMEM((radial, azimuth, outs, axial), BF16),
            pltpu.VMEM((radial, azimuth, outs, axial), BF16),
            pltpu.VMEM((radial, azimuth, channels, axial), BF16),
            pltpu.VMEM((azimuth, radial * axial, 3 * LANES), BF16),
            pltpu.VMEM((3, 3 * channels, 3 * LANES), F32),
            pltpu.VMEM((outs, axial), F32),
            pltpu.VMEM((rows, LANES + 3 * span), BF16),
            pltpu.VMEM((dps, rows, LANES + 3 * span), BF16),
            pltpu.VMEM((3 * outs, 9 * channels), BF16),
            pltpu.VMEM((3 * channels, 9 * outs), BF16),
            pltpu.VMEM((outs, LANES), F32),
            pltpu.VMEM((dps, peers, rows, width), BF16),
            pltpu.VMEM((dps, peers, rows, width), BF16),
            pltpu.VMEM((peers, rows, width), BF16),
            pltpu.VMEM((peers, rows, width), BF16),
            pltpu.VMEM((peers, rows, width), BF16),
            dma((8,)), dma((8,)), dma((8,)), dma((8,)),
            dma((dps,)), dma((dps,)), dma((dps,)), dma((dps,)),
            dma((peers,)), dma((peers,)), dma((peers,)), dma((peers,)),
            dma, dma((radial,)), dma((radial,)),
        ],
        compiler_params=pltpu.CompilerParams(
            vmem_limit_bytes=VMEM_LIMIT, collective_id=0, has_side_effects=True
        ),
    )(inputs[0], weight, bias[None], cotangent[0])
    output = output.transpose(2, 0, 1, 3)[None]
    input_grad = input_grad.transpose(2, 0, 1, 3)[None]
    return output, input_grad, weight_grad, bias_grad[0]


def solution(mesh):
    field_spec = P("dp", None, "rad", "azi", None)
    return jax.shard_map(
        on_device,
        mesh=mesh,
        in_specs=(field_spec, P("dp", None), P("dp"), field_spec),
        out_specs=(field_spec, field_spec, P("dp", None), P("dp")),
        check_vma=False,
    )
```

```python
import functools

import jax
import jax.numpy as jnp
from jax import lax
from jax.experimental import pallas as pl
from jax.experimental.pallas import tpu as pltpu
from jax.sharding import PartitionSpec as P

inverse_scale = 1.0 / 1024.0
VMEM_LIMIT = 60 * 1024 * 1024
LANES = 128
MESH = pl.DeviceIdType.MESH
F32, BF16 = jnp.float32, jnp.bfloat16


def shift(value, step, axis):
    extent = value.shape[axis]
    place = lax.broadcasted_iota(jnp.int32, value.shape, axis)
    edge = 0 if step == 1 else extent - 1
    return jnp.where(place == edge, 0.0, pltpu.roll(value, step % extent, axis))


def columns(cells, r, a):
    return jnp.concatenate([cells[r + i, a + j] for i in range(3) for j in range(3)], axis=0)


def convolve(weight, cells, r, a):
    stacked = jnp.dot(weight, columns(cells, r, a), preferred_element_type=F32)
    rows = stacked.shape[0] // 3
    return (
        stacked[rows:2 * rows]
        + shift(stacked[:rows], 1, 1)
        + shift(stacked[2 * rows:], -1, 1)
    )


class Halo:
    def __init__(self, cells, send, recv):
        self.cells, self.send, self.recv = cells, send, recv
        self.radial, self.azimuth = cells.shape[0] - 2, cells.shape[1] - 2
        self.rad, self.rads = lax.axis_index("rad"), lax.axis_size("rad")
        azi, azis = lax.axis_index("azi"), lax.axis_size("azi")
        self.next, self.prev = lax.rem(azi + 1, azis), lax.rem(azi + azis - 1, azis)

    def copy(self, slot, source, target, where):
        return pltpu.make_async_remote_copy(
            src_ref=source, dst_ref=target, send_sem=self.send.at[slot],
            recv_sem=self.recv.at[slot], device_id=where, device_id_type=MESH,
        )

    def azi_copies(self, first, rows):
        cells, last = self.cells, self.azimuth
        return [
            self.copy(first, cells.at[rows, last], cells.at[rows, 0], {"azi": self.next}),
            self.copy(first + 1, cells.at[rows, 1], cells.at[rows, last + 1], {"azi": self.prev}),
        ]

    def main(self):
        return self.azi_copies(0, pl.ds(1, self.radial))

    def up(self):
        span = pl.ds(1, self.azimuth)
        return self.copy(2, self.cells.at[self.radial, span], self.cells.at[0, span], {"rad": self.rad + 1})

    def down(self):
        span = pl.ds(1, self.azimuth)
        return self.copy(
            3, self.cells.at[1, span], self.cells.at[self.radial + 1, span], {"rad": self.rad - 1}
        )

    def start_rad(self):
        @pl.when(self.rad < self.rads - 1)
        def _():
            self.up().start()

        @pl.when(self.rad > 0)
        def _():
            self.down().start()

    def start_main(self):
        for copy in self.main():
            copy.start()

    def wait_main(self):
        for copy in self.main():
            copy.wait()

    def finish_rim(self):
        @pl.when(self.rad > 0)
        def _():
            self.up().wait_recv()
            for copy in self.azi_copies(4, 0):
                copy.start()

        @pl.when(self.rad < self.rads - 1)
        def _():
            self.down().wait_recv()
            for copy in self.azi_copies(6, self.radial + 1):
                copy.start()

        @pl.when(self.rad == 0)
        def _():
            self.cells[0] = jnp.zeros(self.cells.shape[1:], BF16)

        @pl.when(self.rad == self.rads - 1)
        def _():
            self.cells[self.radial + 1] = jnp.zeros(self.cells.shape[1:], BF16)

        @pl.when(self.rad > 0)
        def _():
            self.down().wait_send()
            for copy in self.azi_copies(4, 0):
                copy.wait()

        @pl.when(self.rad < self.rads - 1)
        def _():
            self.up().wait_send()
            for copy in self.azi_copies(6, self.radial + 1):
                copy.wait()


def kernel(
    field, weight, bias, cotangent,
    output, input_grad, weight_grad, bias_grad,
    cells, dcells, given, turned, result, back_result, dturned, total, bias_total,
    mine, slots, fwd_weight, back_weight, bias_column, part_out, part_in, piece_out, piece_in, final,
    halo_send, halo_recv, dhalo_send, dhalo_recv, w_send, w_recv, p_send, p_recv, q_send, q_recv, f_send, f_recv,
    in_sem, out_sem, back_sem,
):
    channels, radial, azimuth, axial = field.shape
    dp, dps = lax.axis_index("dp"), lax.axis_size("dp")
    rad, azi, azis = lax.axis_index("rad"), lax.axis_index("azi"), lax.axis_size("azi")
    peers = lax.axis_size("rad") * azis
    me = rad * azis + azi
    rows, depth = weight.shape
    outs = rows * dps
    block = depth // 27
    width = final.shape[2]
    span = (mine.shape[1] - LANES) // 3

    def group(k):
        return lax.rem(dp + k, dps)

    def peer(k):
        other = lax.rem(me + k, peers)
        return {"rad": other // azis, "azi": lax.rem(other, azis)}

    def out_copy(r):
        return pltpu.make_async_copy(result.at[r], output.at[r], out_sem.at[r])

    def back_copy(r):
        return pltpu.make_async_copy(back_result.at[r], input_grad.at[r], back_sem.at[r])

    barrier = pltpu.get_barrier_semaphore()

    given_copy = pltpu.make_async_copy(cotangent, given, in_sem)
    given_copy.start()

    @pl.loop(1, dps)
    def _(k):
        pl.semaphore_signal(barrier, inc=1, device_id={"dp": group(k)}, device_id_type=MESH)

    @pl.loop(1, peers)
    def _(k):
        pl.semaphore_signal(barrier, inc=1, device_id=peer(k), device_id_type=MESH)

    own = weight[...].astype(F32)
    pad = jnp.zeros((rows, span - 9 * block), F32)
    for k in range(3):
        parts = [own[:, t * block:(t + 1) * block] for t in range(k, 27, 3)]
        mine[:, LANES + k * span:LANES + (k + 1) * span] = jnp.concatenate(parts + [pad], axis=1).astype(BF16)
    row = lax.broadcasted_iota(jnp.int32, (rows, rows), 0)
    col = lax.broadcasted_iota(jnp.int32, (rows, rows), 1)
    column = jnp.sum(jnp.where(row == col, bias[...].astype(F32), 0.0), axis=1, keepdims=True)
    mine[:, :LANES] = jnp.broadcast_to(column, (rows, LANES)).astype(BF16)

    def turn_row(r):
        cells[r + 1, pl.ds(1, azimuth)] = jnp.swapaxes(field[:, r], 0, 1)

    turn_row(0)
    turn_row(radial - 1)
    pl.semaphore_wait(barrier, dps + peers - 2)

    def w_copy(k):
        return pltpu.make_async_remote_copy(
            src_ref=mine, dst_ref=slots.at[dp], send_sem=w_send.at[k], recv_sem=w_recv.at[k],
            device_id={"dp": group(k)}, device_id_type=MESH,
        )

    halo = Halo(cells, halo_send, halo_recv)

    @pl.loop(1, dps)
    def _(k):
        w_copy(k).start()

    halo.start_rad()

    @pl.loop(1, radial - 1)
    def _(r):
        turn_row(r)

    halo.start_main()
    slots[dp] = mine[...]
    total[...] = jnp.zeros_like(total)
    bias_total[...] = jnp.zeros_like(bias_total)
    given_copy.wait()

    @pl.loop(0, radial)
    def _(r):
        turned[r] = jnp.swapaxes(given[:, r], 0, 1)

    halo.wait_main()

    @pl.loop(1, dps)
    def _(k):
        w_copy(k).wait()

    gathered = jnp.concatenate([slots[g].astype(F32) for g in range(dps)], axis=0)
    bias_column[...] = gathered[:, :LANES]
    for k in range(3):
        start = LANES + k * span
        part = gathered[:, start:start + 9 * block]
        fwd_weight[k * outs:(k + 1) * outs] = part.astype(BF16)
        flipped = [part[:, t * block:(t + 1) * block] for t in reversed(range(9))]
        back_weight[(2 - k) * channels:(3 - k) * channels] = (
            jnp.concatenate(flipped, axis=0).T.astype(BF16)
        )

    @pl.loop(0, radial)
    def _(n):
        r = lax.rem(n + 1, radial)

        @pl.when(n == radial - 2)
        def _():
            halo.finish_rim()

        @pl.loop(0, azimuth // 2)
        def _(pair):
            for p in range(2):
                a = 2 * pair + p
                preact = convolve(fwd_weight[...], cells, r, a) + bias_column[:, :1]
                gate = 0.5 * jnp.tanh(0.5 * preact) + 0.5
                result[r, a] = (preact * gate).astype(BF16)
                d = turned[r, a].astype(F32) * gate * (1.0 + preact * (1.0 - gate))
                d16 = d.astype(BF16)
                d = d16.astype(F32)
                dcells[r + 1, a + 1] = d16
                bias_total[...] += d
                flat = jnp.concatenate([d, jnp.zeros((LANES - outs, axial), F32)], axis=0).T
                dturned[a, pl.ds(pl.multiple_of(r * axial, axial), axial)] = jnp.concatenate(
                    [shift(flat, -1, 0), flat, shift(flat, 1, 0)], axis=1
                ).astype(BF16)

        out_copy(r).start()

    dhalo = Halo(dcells, dhalo_send, dhalo_recv)
    dhalo.start_rad()
    dhalo.start_main()

    def p_copy(i, k):
        return pltpu.make_async_remote_copy(
            src_ref=part_out.at[i, group(k)], dst_ref=part_in.at[i, k], send_sem=p_send.at[i, k],
            recv_sem=p_recv.at[i, k], device_id={"dp": group(k)}, device_id_type=MESH,
        )

    third = 9 * block
    bias_sum = jnp.sum(bias_total[...], axis=1, keepdims=True) * inverse_scale
    for i in range(3):
        @pl.loop(0, azimuth)
        def _(a):
            left = jnp.concatenate(
                [jnp.concatenate([cells[r + i, a + j] for j in range(3)], axis=0) for r in range(radial)],
                axis=1,
            )
            total[i] += jnp.dot(left, dturned[a], preferred_element_type=F32)

        taps = [
            total[i, j * channels:(j + 1) * channels, k * LANES:(k + 1) * LANES]
            for j in range(3) for k in range(3)
        ]
        grads = jnp.concatenate(taps, axis=0).T[:outs] * inverse_scale
        grads = jnp.concatenate([grads, jnp.broadcast_to(bias_sum, (outs, span - third))], axis=1)
        for g in range(dps):
            part_out[i, g] = grads[g * rows:(g + 1) * rows].astype(BF16)

        @pl.loop(1, dps)
        def _(k):
            p_copy(i, k).start()

    def q_copy(k):
        return pltpu.make_async_remote_copy(
            src_ref=piece_out.at[lax.rem(me + k, peers)], dst_ref=piece_in.at[k], send_sem=q_send.at[k],
            recv_sem=q_recv.at[k], device_id=peer(k), device_id_type=MESH,
        )

    def f_copy(k):
        return pltpu.make_async_remote_copy(
            src_ref=final.at[me], dst_ref=final.at[me], send_sem=f_send.at[k],
            recv_sem=f_recv.at[k], device_id=peer(k), device_id_type=MESH,
        )

    dhalo.wait_main()
    pairs = azimuth // 2
    steps = radial * pairs

    @pl.loop(0, steps)
    def _(step):
        r = lax.rem(step // pairs + 1, radial)
        pair = lax.rem(step, pairs)

        @pl.when(step == (radial - 2) * pairs)
        def _():
            dhalo.finish_rim()

        @pl.when(step == 3 * steps // 8)
        def _():
            terms = []
            for i in range(3):
                @pl.loop(1, dps)
                def _(k):
                    p_copy(i, k).wait()

                term = part_out[i, dp].astype(F32)
                for k in range(1, dps):
                    term = term + part_in[i, k].astype(F32)
                terms.append(term)
            spare = peers * width - 3 * span
            if spare:
                terms.append(jnp.zeros((rows, spare), F32))
            terms = jnp.concatenate(terms, axis=1).astype(BF16)
            for p in range(peers):
                piece_out[p] = terms[:, p * width:(p + 1) * width]

            @pl.loop(1, peers)
            def _(k):
                q_copy(k).start()

        @pl.when(step == 11 * steps // 16)
        def _():
            @pl.loop(1, peers)
            def _(k):
                q_copy(k).wait()

            term = piece_out[me].astype(F32)
            for k in range(1, peers):
                term = term + piece_in[k].astype(F32)
            final[me] = term.astype(BF16)

            @pl.loop(1, peers)
            def _(k):
                f_copy(k).start()

        for p in range(2):
            a = 2 * pair + p
            back_result[r, a] = convolve(back_weight[...], dcells, r, a).astype(BF16)

        @pl.when(pair == pairs - 1)
        def _():
            back_copy(r).start()

    @pl.loop(1, peers)
    def _(k):
        f_copy(k).wait()

    used = -(-3 * span // width)
    whole = jnp.concatenate([final[p].astype(F32) for p in range(used)], axis=1)
    weight_grad[...] = jnp.concatenate(
        [whole[:, i * span:i * span + third] for i in range(3)], axis=1
    )
    column = whole[:, 2 * span + third:2 * span + third + 1]
    bias_grad[...] = jnp.sum(jnp.where(row == col, column, 0.0), axis=0, keepdims=True)

    @pl.loop(0, radial)
    def _(r):
        out_copy(r).wait()
        back_copy(r).wait()


def on_device(inputs, weight, bias, cotangent):
    _, channels, radial, azimuth, axial = inputs.shape
    rows, depth = weight.shape
    dps, peers = lax.axis_size("dp"), lax.axis_size("rad") * lax.axis_size("azi")
    outs = rows * dps
    span = -(-(depth // 3 + 1) // LANES) * LANES
    width = -(-3 * span // LANES // peers) * LANES
    vmem = pl.BlockSpec(memory_space=pltpu.VMEM)
    anywhere = pl.BlockSpec(memory_space=pl.ANY)
    shape = jax.ShapeDtypeStruct
    dma = pltpu.SemaphoreType.DMA
    output, input_grad, weight_grad, bias_grad = pl.pallas_call(
        kernel,
        out_shape=(
            shape((radial, azimuth, outs, axial), BF16),
            shape((radial, azimuth, channels, axial), BF16),
            shape((rows, depth), F32),
            shape((1, rows), F32),
        ),
        in_specs=[vmem] * 3 + [anywhere],
        out_specs=(anywhere, anywhere, vmem, vmem),
        scratch_shapes=[
            pltpu.VMEM((radial + 2, azimuth + 2, channels, axial), BF16),
            pltpu.VMEM((radial + 2, azimuth + 2, outs, axial), BF16),
            pltpu.VMEM((outs, radial, azimuth, axial), BF16),
            pltpu.VMEM((radial, azimuth, outs, axial), BF16),
            pltpu.VMEM((radial, azimuth, outs, axial), BF16),
            pltpu.VMEM((radial, azimuth, channels, axial), BF16),
            pltpu.VMEM((azimuth, radial * axial, 3 * LANES), BF16),
            pltpu.VMEM((3, 3 * channels, 3 * LANES), F32),
            pltpu.VMEM((outs, axial), F32),
            pltpu.VMEM((rows, LANES + 3 * span), BF16),
            pltpu.VMEM((dps, rows, LANES + 3 * span), BF16),
            pltpu.VMEM((3 * outs, 9 * channels), BF16),
            pltpu.VMEM((3 * channels, 9 * outs), BF16),
            pltpu.VMEM((outs, LANES), F32),
            pltpu.VMEM((3, dps, rows, span), BF16),
            pltpu.VMEM((3, dps, rows, span), BF16),
            pltpu.VMEM((peers, rows, width), BF16),
            pltpu.VMEM((peers, rows, width), BF16),
            pltpu.VMEM((peers, rows, width), BF16),
            dma((8,)), dma((8,)), dma((8,)), dma((8,)),
            dma((dps,)), dma((dps,)), dma((3, dps)), dma((3, dps)),
            dma((peers,)), dma((peers,)), dma((peers,)), dma((peers,)),
            dma, dma((radial,)), dma((radial,)),
        ],
        compiler_params=pltpu.CompilerParams(
            vmem_limit_bytes=VMEM_LIMIT, collective_id=0, has_side_effects=True
        ),
    )(inputs[0], weight, bias[None], cotangent[0])
    output = output.transpose(2, 0, 1, 3)[None]
    input_grad = input_grad.transpose(2, 0, 1, 3)[None]
    return output, input_grad, weight_grad, bias_grad[0]


def solution(mesh):
    field_spec = P("dp", None, "rad", "azi", None)
    return jax.shard_map(
        on_device,
        mesh=mesh,
        in_specs=(field_spec, P("dp", None), P("dp"), field_spec),
        out_specs=(field_spec, field_spec, P("dp", None), P("dp")),
        check_vma=False,
    )
```

```python
import functools

import jax
import jax.numpy as jnp
from jax import lax
from jax.experimental import pallas as pl
from jax.experimental.pallas import tpu as pltpu
from jax.sharding import PartitionSpec as P

inverse_scale = 1.0 / 1024.0
VMEM_LIMIT = 60 * 1024 * 1024
LANES = 128
MESH = pl.DeviceIdType.MESH
F32, BF16 = jnp.float32, jnp.bfloat16


def shift(value, step, axis):
    extent = value.shape[axis]
    place = lax.broadcasted_iota(jnp.int32, value.shape, axis)
    edge = 0 if step == 1 else extent - 1
    return jnp.where(place == edge, 0.0, pltpu.roll(value, step % extent, axis))


def columns(cells, r, a):
    return jnp.concatenate([cells[r + i, a + j] for i in range(3) for j in range(3)], axis=0)


def convolve(weight, cells, r, a):
    stacked = jnp.dot(weight, columns(cells, r, a), preferred_element_type=F32)
    rows = stacked.shape[0] // 3
    return (
        stacked[rows:2 * rows]
        + shift(stacked[:rows], 1, 1)
        + shift(stacked[2 * rows:], -1, 1)
    )


class Halo:
    def __init__(self, cells, send, recv):
        self.cells, self.send, self.recv = cells, send, recv
        self.radial, self.azimuth = cells.shape[0] - 2, cells.shape[1] - 2
        self.rad, self.rads = lax.axis_index("rad"), lax.axis_size("rad")
        azi, azis = lax.axis_index("azi"), lax.axis_size("azi")
        self.next, self.prev = lax.rem(azi + 1, azis), lax.rem(azi + azis - 1, azis)

    def copy(self, slot, source, target, where):
        return pltpu.make_async_remote_copy(
            src_ref=source, dst_ref=target, send_sem=self.send.at[slot],
            recv_sem=self.recv.at[slot], device_id=where, device_id_type=MESH,
        )

    def azi_copies(self, first, rows):
        cells, last = self.cells, self.azimuth
        return [
            self.copy(first, cells.at[rows, last], cells.at[rows, 0], {"azi": self.next}),
            self.copy(first + 1, cells.at[rows, 1], cells.at[rows, last + 1], {"azi": self.prev}),
        ]

    def main(self):
        return self.azi_copies(0, pl.ds(1, self.radial))

    def up(self):
        span = pl.ds(1, self.azimuth)
        return self.copy(2, self.cells.at[self.radial, span], self.cells.at[0, span], {"rad": self.rad + 1})

    def down(self):
        span = pl.ds(1, self.azimuth)
        return self.copy(
            3, self.cells.at[1, span], self.cells.at[self.radial + 1, span], {"rad": self.rad - 1}
        )

    def start_rad(self):
        @pl.when(self.rad < self.rads - 1)
        def _():
            self.up().start()

        @pl.when(self.rad > 0)
        def _():
            self.down().start()

    def start_main(self):
        for copy in self.main():
            copy.start()

    def wait_main(self):
        for copy in self.main():
            copy.wait()

    def start_corners(self):
        @pl.when(self.rad > 0)
        def _():
            self.up().wait_recv()
            for copy in self.azi_copies(4, 0):
                copy.start()

        @pl.when(self.rad < self.rads - 1)
        def _():
            self.down().wait_recv()
            for copy in self.azi_copies(6, self.radial + 1):
                copy.start()

        @pl.when(self.rad == 0)
        def _():
            self.cells[0] = jnp.zeros(self.cells.shape[1:], BF16)

        @pl.when(self.rad == self.rads - 1)
        def _():
            self.cells[self.radial + 1] = jnp.zeros(self.cells.shape[1:], BF16)

    def wait_corners(self):
        @pl.when(self.rad > 0)
        def _():
            self.down().wait_send()
            for copy in self.azi_copies(4, 0):
                copy.wait()

        @pl.when(self.rad < self.rads - 1)
        def _():
            self.up().wait_send()
            for copy in self.azi_copies(6, self.radial + 1):
                copy.wait()


def kernel(
    field, weight, bias, cotangent,
    output, input_grad, weight_grad, bias_grad,
    cells, dcells, given, turned, result, back_result, dturned, total, bias_total,
    mine, slots, fwd_weight, back_weight, bias_column, part_out, part_in, piece_out, piece_in, final,
    halo_send, halo_recv, dhalo_send, dhalo_recv, w_send, w_recv, p_send, p_recv, q_send, q_recv, f_send, f_recv,
    in_sem, out_sem, back_sem,
):
    channels, radial, azimuth, axial = field.shape
    dp, dps = lax.axis_index("dp"), lax.axis_size("dp")
    rad, azi, azis = lax.axis_index("rad"), lax.axis_index("azi"), lax.axis_size("azi")
    peers = lax.axis_size("rad") * azis
    me = rad * azis + azi
    rows, depth = weight.shape
    outs = rows * dps
    block = depth // 27
    width = final.shape[2]
    span = (mine.shape[1] - LANES) // 3

    def group(k):
        return lax.rem(dp + k, dps)

    def peer(k):
        other = lax.rem(me + k, peers)
        return {"rad": other // azis, "azi": lax.rem(other, azis)}

    def out_copy(r):
        return pltpu.make_async_copy(result.at[r], output.at[r], out_sem.at[r])

    def back_copy(r):
        return pltpu.make_async_copy(back_result.at[r], input_grad.at[r], back_sem.at[r])

    barrier = pltpu.get_barrier_semaphore()

    given_copy = pltpu.make_async_copy(cotangent, given, in_sem)
    given_copy.start()

    @pl.loop(1, dps)
    def _(k):
        pl.semaphore_signal(barrier, inc=1, device_id={"dp": group(k)}, device_id_type=MESH)

    @pl.loop(1, peers)
    def _(k):
        pl.semaphore_signal(barrier, inc=1, device_id=peer(k), device_id_type=MESH)

    own = weight[...].astype(F32)
    pad = jnp.zeros((rows, span - 9 * block), F32)
    for k in range(3):
        parts = [own[:, t * block:(t + 1) * block] for t in range(k, 27, 3)]
        mine[:, LANES + k * span:LANES + (k + 1) * span] = jnp.concatenate(parts + [pad], axis=1).astype(BF16)
    row = lax.broadcasted_iota(jnp.int32, (rows, rows), 0)
    col = lax.broadcasted_iota(jnp.int32, (rows, rows), 1)
    column = jnp.sum(jnp.where(row == col, bias[...].astype(F32), 0.0), axis=1, keepdims=True)
    mine[:, :LANES] = jnp.broadcast_to(column, (rows, LANES)).astype(BF16)

    def turn_row(r):
        cells[r + 1, pl.ds(1, azimuth)] = jnp.swapaxes(field[:, r], 0, 1)

    turn_row(0)
    turn_row(radial - 1)
    pl.semaphore_wait(barrier, dps + peers - 2)

    def w_copy(k):
        return pltpu.make_async_remote_copy(
            src_ref=mine, dst_ref=slots.at[dp], send_sem=w_send.at[k], recv_sem=w_recv.at[k],
            device_id={"dp": group(k)}, device_id_type=MESH,
        )

    halo = Halo(cells, halo_send, halo_recv)

    @pl.loop(1, dps)
    def _(k):
        w_copy(k).start()

    halo.start_rad()

    @pl.loop(1, radial - 1)
    def _(r):
        turn_row(r)

    halo.start_main()
    slots[dp] = mine[...]
    total[...] = jnp.zeros_like(total)
    bias_total[...] = jnp.zeros_like(bias_total)
    given_copy.wait()

    @pl.loop(0, radial)
    def _(r):
        turned[r] = jnp.swapaxes(given[:, r], 0, 1)

    halo.wait_main()

    @pl.loop(1, dps)
    def _(k):
        w_copy(k).wait()

    gathered = jnp.concatenate([slots[g].astype(F32) for g in range(dps)], axis=0)
    bias_column[...] = gathered[:, :LANES]
    for k in range(3):
        start = LANES + k * span
        part = gathered[:, start:start + 9 * block]
        fwd_weight[k * outs:(k + 1) * outs] = part.astype(BF16)
        flipped = [part[:, t * block:(t + 1) * block] for t in reversed(range(9))]
        back_weight[(2 - k) * channels:(3 - k) * channels] = (
            jnp.concatenate(flipped, axis=0).T.astype(BF16)
        )

    @pl.loop(0, radial)
    def _(n):
        r = lax.rem(n + 1, radial)

        @pl.when(n == max(radial - 3, 0))
        def _():
            halo.start_corners()

        @pl.when(n == radial - 2)
        def _():
            halo.wait_corners()

        @pl.loop(0, azimuth // 2)
        def _(pair):
            for p in range(2):
                a = 2 * pair + p
                preact = convolve(fwd_weight[...], cells, r, a) + bias_column[:, :1]
                gate = 0.5 * jnp.tanh(0.5 * preact) + 0.5
                result[r, a] = (preact * gate).astype(BF16)
                d = turned[r, a].astype(F32) * gate * (1.0 + preact * (1.0 - gate))
                d16 = d.astype(BF16)
                d = d16.astype(F32)
                dcells[r + 1, a + 1] = d16
                bias_total[...] += d
                flat = jnp.concatenate([d, jnp.zeros((LANES - outs, axial), F32)], axis=0).T
                dturned[a, pl.ds(pl.multiple_of(r * axial, axial), axial)] = jnp.concatenate(
                    [shift(flat, -1, 0), flat, shift(flat, 1, 0)], axis=1
                ).astype(BF16)

        out_copy(r).start()

    dhalo = Halo(dcells, dhalo_send, dhalo_recv)
    dhalo.start_rad()
    dhalo.start_main()

    def p_copy(i, k):
        return pltpu.make_async_remote_copy(
            src_ref=part_out.at[i, group(k)], dst_ref=part_in.at[i, k], send_sem=p_send.at[i, k],
            recv_sem=p_recv.at[i, k], device_id={"dp": group(k)}, device_id_type=MESH,
        )

    third = 9 * block
    bias_sum = jnp.sum(bias_total[...], axis=1, keepdims=True) * inverse_scale
    for i in range(3):
        @pl.loop(0, azimuth)
        def _(a):
            left = jnp.concatenate(
                [jnp.concatenate([cells[r + i, a + j] for j in range(3)], axis=0) for r in range(radial)],
                axis=1,
            )
            total[i] += jnp.dot(left, dturned[a], preferred_element_type=F32)

        taps = [
            total[i, j * channels:(j + 1) * channels, k * LANES:(k + 1) * LANES]
            for j in range(3) for k in range(3)
        ]
        grads = jnp.concatenate(taps, axis=0).T[:outs] * inverse_scale
        grads = jnp.concatenate([grads, jnp.broadcast_to(bias_sum, (outs, span - third))], axis=1)
        for g in range(dps):
            part_out[i, g] = grads[g * rows:(g + 1) * rows].astype(BF16)

        @pl.loop(1, dps)
        def _(k):
            p_copy(i, k).start()

    def q_copy(k):
        return pltpu.make_async_remote_copy(
            src_ref=piece_out.at[lax.rem(me + k, peers)], dst_ref=piece_in.at[k], send_sem=q_send.at[k],
            recv_sem=q_recv.at[k], device_id=peer(k), device_id_type=MESH,
        )

    def f_copy(k):
        return pltpu.make_async_remote_copy(
            src_ref=final.at[me], dst_ref=final.at[me], send_sem=f_send.at[k],
            recv_sem=f_recv.at[k], device_id=peer(k), device_id_type=MESH,
        )

    dhalo.wait_main()
    pairs = azimuth // 2
    steps = radial * pairs

    @pl.loop(0, steps)
    def _(step):
        r = lax.rem(step // pairs + 1, radial)
        pair = lax.rem(step, pairs)

        @pl.when(step == max(radial - 3, 0) * pairs)
        def _():
            dhalo.start_corners()

        @pl.when(step == (radial - 2) * pairs)
        def _():
            dhalo.wait_corners()

        @pl.when(step == 3 * steps // 8)
        def _():
            terms = []
            for i in range(3):
                @pl.loop(1, dps)
                def _(k):
                    p_copy(i, k).wait()

                term = part_out[i, dp].astype(F32)
                for k in range(1, dps):
                    term = term + part_in[i, k].astype(F32)
                terms.append(term)
            spare = peers * width - 3 * span
            if spare:
                terms.append(jnp.zeros((rows, spare), F32))
            terms = jnp.concatenate(terms, axis=1).astype(BF16)
            for p in range(peers):
                piece_out[p] = terms[:, p * width:(p + 1) * width]

            @pl.loop(1, peers)
            def _(k):
                q_copy(k).start()

        @pl.when(step == 11 * steps // 16)
        def _():
            @pl.loop(1, peers)
            def _(k):
                q_copy(k).wait()

            term = piece_out[me].astype(F32)
            for k in range(1, peers):
                term = term + piece_in[k].astype(F32)
            final[me] = term.astype(BF16)

            @pl.loop(1, peers)
            def _(k):
                f_copy(k).start()

        for p in range(2):
            a = 2 * pair + p
            back_result[r, a] = convolve(back_weight[...], dcells, r, a).astype(BF16)

        @pl.when(pair == pairs - 1)
        def _():
            back_copy(r).start()

    @pl.loop(1, peers)
    def _(k):
        f_copy(k).wait()

    used = -(-3 * span // width)
    whole = jnp.concatenate([final[p].astype(F32) for p in range(used)], axis=1)
    weight_grad[...] = jnp.concatenate(
        [whole[:, i * span:i * span + third] for i in range(3)], axis=1
    )
    column = whole[:, 2 * span + third:2 * span + third + 1]
    bias_grad[...] = jnp.sum(jnp.where(row == col, column, 0.0), axis=0, keepdims=True)

    @pl.loop(0, radial)
    def _(r):
        out_copy(r).wait()
        back_copy(r).wait()


def turn_kernel(output, input_grad, weight_grad, bias_grad, output_to, input_to, weight_to, bias_to):
    output_to[:, 0] = jnp.swapaxes(output[0], 0, 1)
    input_to[:, 0] = jnp.swapaxes(input_grad[0], 0, 1)

    @pl.when(pl.program_id(0) == 0)
    def _():
        weight_to[...] = weight_grad[...]
        bias_to[...] = bias_grad[...]


def on_device(inputs, weight, bias, cotangent):
    _, channels, radial, azimuth, axial = inputs.shape
    rows, depth = weight.shape
    dps, peers = lax.axis_size("dp"), lax.axis_size("rad") * lax.axis_size("azi")
    outs = rows * dps
    span = -(-(depth // 3 + 1) // LANES) * LANES
    width = -(-3 * span // LANES // peers) * LANES
    vmem = pl.BlockSpec(memory_space=pltpu.VMEM)
    anywhere = pl.BlockSpec(memory_space=pl.ANY)
    shape = jax.ShapeDtypeStruct
    dma = pltpu.SemaphoreType.DMA
    output, input_grad, weight_grad, bias_grad = pl.pallas_call(
        kernel,
        out_shape=(
            shape((radial, azimuth, outs, axial), BF16),
            shape((radial, azimuth, channels, axial), BF16),
            shape((rows, depth), F32),
            shape((1, rows), F32),
        ),
        in_specs=[vmem] * 3 + [anywhere],
        out_specs=(anywhere, anywhere, vmem, vmem),
        scratch_shapes=[
            pltpu.VMEM((radial + 2, azimuth + 2, channels, axial), BF16),
            pltpu.VMEM((radial + 2, azimuth + 2, outs, axial), BF16),
            pltpu.VMEM((outs, radial, azimuth, axial), BF16),
            pltpu.VMEM((radial, azimuth, outs, axial), BF16),
            pltpu.VMEM((radial, azimuth, outs, axial), BF16),
            pltpu.VMEM((radial, azimuth, channels, axial), BF16),
            pltpu.VMEM((azimuth, radial * axial, 3 * LANES), BF16),
            pltpu.VMEM((3, 3 * channels, 3 * LANES), F32),
            pltpu.VMEM((outs, axial), F32),
            pltpu.VMEM((rows, LANES + 3 * span), BF16),
            pltpu.VMEM((dps, rows, LANES + 3 * span), BF16),
            pltpu.VMEM((3 * outs, 9 * channels), BF16),
            pltpu.VMEM((3 * channels, 9 * outs), BF16),
            pltpu.VMEM((outs, LANES), F32),
            pltpu.VMEM((3, dps, rows, span), BF16),
            pltpu.VMEM((3, dps, rows, span), BF16),
            pltpu.VMEM((peers, rows, width), BF16),
            pltpu.VMEM((peers, rows, width), BF16),
            pltpu.VMEM((peers, rows, width), BF16),
            dma((8,)), dma((8,)), dma((8,)), dma((8,)),
            dma((dps,)), dma((dps,)), dma((3, dps)), dma((3, dps)),
            dma((peers,)), dma((peers,)), dma((peers,)), dma((peers,)),
            dma, dma((radial,)), dma((radial,)),
        ],
        compiler_params=pltpu.CompilerParams(
            vmem_limit_bytes=VMEM_LIMIT, collective_id=0, has_side_effects=True
        ),
    )(inputs[0], weight, bias[None], cotangent[0])
    row_in = pl.BlockSpec((1, azimuth, channels, axial), lambda r: (r, 0, 0, 0))
    row_out = pl.BlockSpec((channels, 1, azimuth, axial), lambda r: (0, r, 0, 0))
    weight_spec = pl.BlockSpec((rows, depth), lambda r: (0, 0))
    bias_spec = pl.BlockSpec((1, rows), lambda r: (0, 0))
    output, input_grad, weight_grad, bias_grad = pl.pallas_call(
        turn_kernel,
        grid=(radial,),
        out_shape=(
            shape((outs, radial, azimuth, axial), BF16),
            shape((channels, radial, azimuth, axial), BF16),
            shape((rows, depth), F32),
            shape((1, rows), F32),
        ),
        in_specs=[row_in, row_in, weight_spec, bias_spec],
        out_specs=(row_out, row_out, weight_spec, bias_spec),
        compiler_params=pltpu.CompilerParams(vmem_limit_bytes=63 * 1024 * 1024),
    )(output, input_grad, weight_grad, bias_grad)
    return output[None], input_grad[None], weight_grad, bias_grad[0]


def solution(mesh):
    field_spec = P("dp", None, "rad", "azi", None)
    return jax.shard_map(
        on_device,
        mesh=mesh,
        in_specs=(field_spec, P("dp", None), P("dp"), field_spec),
        out_specs=(field_spec, field_spec, P("dp", None), P("dp")),
        check_vma=False,
    )
```

```python
import functools

import jax
import jax.numpy as jnp
from jax import lax
from jax.experimental import pallas as pl
from jax.experimental.pallas import tpu as pltpu
from jax.sharding import PartitionSpec as P

inverse_scale = 1.0 / 1024.0
VMEM_LIMIT = 60 * 1024 * 1024
LANES = 128
MESH = pl.DeviceIdType.MESH
F32, BF16 = jnp.float32, jnp.bfloat16


def shift(value, step, axis):
    extent = value.shape[axis]
    place = lax.broadcasted_iota(jnp.int32, value.shape, axis)
    edge = 0 if step == 1 else extent - 1
    return jnp.where(place == edge, 0.0, pltpu.roll(value, step % extent, axis))


def columns(cells, r, a):
    return jnp.concatenate([cells[r + i, a + j] for i in range(3) for j in range(3)], axis=0)


def convolve(weight, cells, r, a):
    stacked = jnp.dot(weight, columns(cells, r, a), preferred_element_type=F32)
    rows = stacked.shape[0] // 3
    return (
        stacked[rows:2 * rows]
        + shift(stacked[:rows], 1, 1)
        + shift(stacked[2 * rows:], -1, 1)
    )


class Halo:
    def __init__(self, cells, send, recv):
        self.cells, self.send, self.recv = cells, send, recv
        self.radial, self.azimuth = cells.shape[0] - 2, cells.shape[1] - 2
        self.rad, self.rads = lax.axis_index("rad"), lax.axis_size("rad")
        azi, azis = lax.axis_index("azi"), lax.axis_size("azi")
        self.next, self.prev = lax.rem(azi + 1, azis), lax.rem(azi + azis - 1, azis)

    def copy(self, slot, source, target, where):
        return pltpu.make_async_remote_copy(
            src_ref=source, dst_ref=target, send_sem=self.send.at[slot],
            recv_sem=self.recv.at[slot], device_id=where, device_id_type=MESH,
        )

    def azi_copies(self, first, rows):
        cells, last = self.cells, self.azimuth
        return [
            self.copy(first, cells.at[rows, last], cells.at[rows, 0], {"azi": self.next}),
            self.copy(first + 1, cells.at[rows, 1], cells.at[rows, last + 1], {"azi": self.prev}),
        ]

    def main(self):
        return self.azi_copies(0, pl.ds(1, self.radial))

    def up(self):
        span = pl.ds(1, self.azimuth)
        return self.copy(2, self.cells.at[self.radial, span], self.cells.at[0, span], {"rad": self.rad + 1})

    def down(self):
        span = pl.ds(1, self.azimuth)
        return self.copy(
            3, self.cells.at[1, span], self.cells.at[self.radial + 1, span], {"rad": self.rad - 1}
        )

    def start_rad(self):
        @pl.when(self.rad < self.rads - 1)
        def _():
            self.up().start()

        @pl.when(self.rad > 0)
        def _():
            self.down().start()

    def start_main(self):
        for copy in self.main():
            copy.start()

    def wait_main(self):
        for copy in self.main():
            copy.wait()

    def start_corners(self):
        @pl.when(self.rad > 0)
        def _():
            self.up().wait_recv()
            for copy in self.azi_copies(4, 0):
                copy.start()

        @pl.when(self.rad < self.rads - 1)
        def _():
            self.down().wait_recv()
            for copy in self.azi_copies(6, self.radial + 1):
                copy.start()

        @pl.when(self.rad == 0)
        def _():
            self.cells[0] = jnp.zeros(self.cells.shape[1:], BF16)

        @pl.when(self.rad == self.rads - 1)
        def _():
            self.cells[self.radial + 1] = jnp.zeros(self.cells.shape[1:], BF16)

    def wait_corners(self):
        @pl.when(self.rad > 0)
        def _():
            self.down().wait_send()
            for copy in self.azi_copies(4, 0):
                copy.wait()

        @pl.when(self.rad < self.rads - 1)
        def _():
            self.up().wait_send()
            for copy in self.azi_copies(6, self.radial + 1):
                copy.wait()


def kernel(
    field, weight, bias, cotangent,
    output, input_grad, weight_grad, bias_grad,
    cells, dcells, given, turned, result, back_result, dturned, total, bias_total,
    mine, slots, fwd_weight, back_weight, bias_column, part_out, part_in, piece_out, piece_in, final,
    halo_send, halo_recv, dhalo_send, dhalo_recv, w_send, w_recv, p_send, p_recv, q_send, q_recv, f_send, f_recv,
    in_sem, out_sem, back_sem,
):
    channels, radial, azimuth, axial = field.shape
    dp, dps = lax.axis_index("dp"), lax.axis_size("dp")
    rad, azi, azis = lax.axis_index("rad"), lax.axis_index("azi"), lax.axis_size("azi")
    peers = lax.axis_size("rad") * azis
    me = rad * azis + azi
    rows, depth = weight.shape
    outs = rows * dps
    block = depth // 27
    width = final.shape[2]
    batch = max(b for b in (1, 2, 4) if azimuth % b == 0)
    span = (mine.shape[1] - LANES) // 3

    def group(k):
        return lax.rem(dp + k, dps)

    def peer(k):
        other = lax.rem(me + k, peers)
        return {"rad": other // azis, "azi": lax.rem(other, azis)}

    def out_copy(r):
        return pltpu.make_async_copy(result.at[r], output.at[r], out_sem.at[r])

    def back_copy(r):
        return pltpu.make_async_copy(back_result.at[r], input_grad.at[r], back_sem.at[r])

    barrier = pltpu.get_barrier_semaphore()

    given_copy = pltpu.make_async_copy(cotangent, given, in_sem)
    given_copy.start()

    @pl.loop(1, dps)
    def _(k):
        pl.semaphore_signal(barrier, inc=1, device_id={"dp": group(k)}, device_id_type=MESH)

    @pl.loop(1, peers)
    def _(k):
        pl.semaphore_signal(barrier, inc=1, device_id=peer(k), device_id_type=MESH)

    own = weight[...].astype(F32)
    pad = jnp.zeros((rows, span - 9 * block), F32)
    for k in range(3):
        parts = [own[:, t * block:(t + 1) * block] for t in range(k, 27, 3)]
        mine[:, LANES + k * span:LANES + (k + 1) * span] = jnp.concatenate(parts + [pad], axis=1).astype(BF16)
    row = lax.broadcasted_iota(jnp.int32, (rows, rows), 0)
    col = lax.broadcasted_iota(jnp.int32, (rows, rows), 1)
    column = jnp.sum(jnp.where(row == col, bias[...].astype(F32), 0.0), axis=1, keepdims=True)
    mine[:, :LANES] = jnp.broadcast_to(column, (rows, LANES)).astype(BF16)

    def turn_row(r):
        cells[r + 1, pl.ds(1, azimuth)] = jnp.swapaxes(field[:, r], 0, 1)

    turn_row(0)
    turn_row(radial - 1)
    pl.semaphore_wait(barrier, dps + peers - 2)

    def w_copy(k):
        return pltpu.make_async_remote_copy(
            src_ref=mine, dst_ref=slots.at[dp], send_sem=w_send.at[k], recv_sem=w_recv.at[k],
            device_id={"dp": group(k)}, device_id_type=MESH,
        )

    halo = Halo(cells, halo_send, halo_recv)

    @pl.loop(1, dps)
    def _(k):
        w_copy(k).start()

    halo.start_rad()

    @pl.loop(1, radial - 1)
    def _(r):
        turn_row(r)

    halo.start_main()
    slots[dp] = mine[...]
    total[...] = jnp.zeros_like(total)
    bias_total[...] = jnp.zeros_like(bias_total)
    given_copy.wait()

    @pl.loop(0, radial)
    def _(r):
        turned[r] = jnp.swapaxes(given[:, r], 0, 1)

    halo.wait_main()

    @pl.loop(1, dps)
    def _(k):
        w_copy(k).wait()

    gathered = jnp.concatenate([slots[g].astype(F32) for g in range(dps)], axis=0)
    bias_column[...] = gathered[:, :LANES]
    for k in range(3):
        start = LANES + k * span
        part = gathered[:, start:start + 9 * block]
        fwd_weight[k * outs:(k + 1) * outs] = part.astype(BF16)
        flipped = [part[:, t * block:(t + 1) * block] for t in reversed(range(9))]
        back_weight[(2 - k) * channels:(3 - k) * channels] = (
            jnp.concatenate(flipped, axis=0).T.astype(BF16)
        )

    @pl.loop(0, radial)
    def _(n):
        r = lax.rem(n + 1, radial)

        @pl.when(n == max(radial - 3, 0))
        def _():
            halo.start_corners()

        @pl.when(n == radial - 2)
        def _():
            halo.wait_corners()

        @pl.loop(0, azimuth // batch)
        def _(part):
            for p in range(batch):
                a = batch * part + p
                preact = convolve(fwd_weight[...], cells, r, a) + bias_column[:, :1]
                gate = 0.5 * jnp.tanh(0.5 * preact) + 0.5
                result[r, a] = (preact * gate).astype(BF16)
                d = turned[r, a].astype(F32) * gate * (1.0 + preact * (1.0 - gate))
                d16 = d.astype(BF16)
                d = d16.astype(F32)
                dcells[r + 1, a + 1] = d16
                bias_total[...] += d
                flat = jnp.concatenate([d, jnp.zeros((LANES - outs, axial), F32)], axis=0).T
                dturned[a, pl.ds(pl.multiple_of(r * axial, axial), axial)] = jnp.concatenate(
                    [shift(flat, -1, 0), flat, shift(flat, 1, 0)], axis=1
                ).astype(BF16)

        out_copy(r).start()

    dhalo = Halo(dcells, dhalo_send, dhalo_recv)
    dhalo.start_rad()
    dhalo.start_main()

    def p_copy(i, k):
        return pltpu.make_async_remote_copy(
            src_ref=part_out.at[i, group(k)], dst_ref=part_in.at[i, k], send_sem=p_send.at[i, k],
            recv_sem=p_recv.at[i, k], device_id={"dp": group(k)}, device_id_type=MESH,
        )

    third = 9 * block
    bias_sum = jnp.sum(bias_total[...], axis=1, keepdims=True) * inverse_scale
    for i in range(3):
        @pl.loop(0, azimuth)
        def _(a):
            left = jnp.concatenate(
                [jnp.concatenate([cells[r + i, a + j] for j in range(3)], axis=0) for r in range(radial)],
                axis=1,
            )
            total[i] += jnp.dot(left, dturned[a], preferred_element_type=F32)

        taps = [
            total[i, j * channels:(j + 1) * channels, k * LANES:(k + 1) * LANES]
            for j in range(3) for k in range(3)
        ]
        grads = jnp.concatenate(taps, axis=0).T[:outs] * inverse_scale
        grads = jnp.concatenate([grads, jnp.broadcast_to(bias_sum, (outs, span - third))], axis=1)
        for g in range(dps):
            part_out[i, g] = grads[g * rows:(g + 1) * rows].astype(BF16)

        @pl.loop(1, dps)
        def _(k):
            p_copy(i, k).start()

    def q_copy(k):
        return pltpu.make_async_remote_copy(
            src_ref=piece_out.at[lax.rem(me + k, peers)], dst_ref=piece_in.at[k], send_sem=q_send.at[k],
            recv_sem=q_recv.at[k], device_id=peer(k), device_id_type=MESH,
        )

    def f_copy(k):
        return pltpu.make_async_remote_copy(
            src_ref=final.at[me], dst_ref=final.at[me], send_sem=f_send.at[k],
            recv_sem=f_recv.at[k], device_id=peer(k), device_id_type=MESH,
        )

    dhalo.wait_main()
    pairs = azimuth // batch
    steps = radial * pairs

    @pl.loop(0, steps)
    def _(step):
        r = lax.rem(step // pairs + 1, radial)
        pair = lax.rem(step, pairs)

        @pl.when(step == max(radial - 3, 0) * pairs)
        def _():
            dhalo.start_corners()

        @pl.when(step == (radial - 2) * pairs)
        def _():
            dhalo.wait_corners()

        @pl.when(step == 3 * steps // 8)
        def _():
            terms = []
            for i in range(3):
                @pl.loop(1, dps)
                def _(k):
                    p_copy(i, k).wait()

                term = part_out[i, dp].astype(F32)
                for k in range(1, dps):
                    term = term + part_in[i, k].astype(F32)
                terms.append(term)
            spare = peers * width - 3 * span
            if spare:
                terms.append(jnp.zeros((rows, spare), F32))
            terms = jnp.concatenate(terms, axis=1).astype(BF16)
            for p in range(peers):
                piece_out[p] = terms[:, p * width:(p + 1) * width]

            @pl.loop(1, peers)
            def _(k):
                q_copy(k).start()

        @pl.when(step == 11 * steps // 16)
        def _():
            @pl.loop(1, peers)
            def _(k):
                q_copy(k).wait()

            term = piece_out[me].astype(F32)
            for k in range(1, peers):
                term = term + piece_in[k].astype(F32)
            final[me] = term.astype(BF16)

            @pl.loop(1, peers)
            def _(k):
                f_copy(k).start()

        for p in range(batch):
            a = batch * pair + p
            back_result[r, a] = convolve(back_weight[...], dcells, r, a).astype(BF16)

        @pl.when(pair == pairs - 1)
        def _():
            back_copy(r).start()

    @pl.loop(1, peers)
    def _(k):
        f_copy(k).wait()

    used = -(-3 * span // width)
    whole = jnp.concatenate([final[p].astype(F32) for p in range(used)], axis=1)
    weight_grad[...] = jnp.concatenate(
        [whole[:, i * span:i * span + third] for i in range(3)], axis=1
    )
    column = whole[:, 2 * span + third:2 * span + third + 1]
    bias_grad[...] = jnp.sum(jnp.where(row == col, column, 0.0), axis=0, keepdims=True)

    @pl.loop(0, radial)
    def _(r):
        out_copy(r).wait()
        back_copy(r).wait()


def turn_kernel(output, input_grad, weight_grad, bias_grad, output_to, input_to, weight_to, bias_to):
    output_to[:, 0] = jnp.swapaxes(output[0], 0, 1)
    input_to[:, 0] = jnp.swapaxes(input_grad[0], 0, 1)

    @pl.when(pl.program_id(0) == 0)
    def _():
        weight_to[...] = weight_grad[...]
        bias_to[...] = bias_grad[...]


def on_device(inputs, weight, bias, cotangent):
    _, channels, radial, azimuth, axial = inputs.shape
    rows, depth = weight.shape
    dps, peers = lax.axis_size("dp"), lax.axis_size("rad") * lax.axis_size("azi")
    outs = rows * dps
    span = -(-(depth // 3 + 1) // LANES) * LANES
    width = -(-3 * span // LANES // peers) * LANES
    vmem = pl.BlockSpec(memory_space=pltpu.VMEM)
    anywhere = pl.BlockSpec(memory_space=pl.ANY)
    shape = jax.ShapeDtypeStruct
    dma = pltpu.SemaphoreType.DMA
    output, input_grad, weight_grad, bias_grad = pl.pallas_call(
        kernel,
        out_shape=(
            shape((radial, azimuth, outs, axial), BF16),
            shape((radial, azimuth, channels, axial), BF16),
            shape((rows, depth), F32),
            shape((1, rows), F32),
        ),
        in_specs=[vmem] * 3 + [anywhere],
        out_specs=(anywhere, anywhere, vmem, vmem),
        scratch_shapes=[
            pltpu.VMEM((radial + 2, azimuth + 2, channels, axial), BF16),
            pltpu.VMEM((radial + 2, azimuth + 2, outs, axial), BF16),
            pltpu.VMEM((outs, radial, azimuth, axial), BF16),
            pltpu.VMEM((radial, azimuth, outs, axial), BF16),
            pltpu.VMEM((radial, azimuth, outs, axial), BF16),
            pltpu.VMEM((radial, azimuth, channels, axial), BF16),
            pltpu.VMEM((azimuth, radial * axial, 3 * LANES), BF16),
            pltpu.VMEM((3, 3 * channels, 3 * LANES), F32),
            pltpu.VMEM((outs, axial), F32),
            pltpu.VMEM((rows, LANES + 3 * span), BF16),
            pltpu.VMEM((dps, rows, LANES + 3 * span), BF16),
            pltpu.VMEM((3 * outs, 9 * channels), BF16),
            pltpu.VMEM((3 * channels, 9 * outs), BF16),
            pltpu.VMEM((outs, LANES), F32),
            pltpu.VMEM((3, dps, rows, span), BF16),
            pltpu.VMEM((3, dps, rows, span), BF16),
            pltpu.VMEM((peers, rows, width), BF16),
            pltpu.VMEM((peers, rows, width), BF16),
            pltpu.VMEM((peers, rows, width), BF16),
            dma((8,)), dma((8,)), dma((8,)), dma((8,)),
            dma((dps,)), dma((dps,)), dma((3, dps)), dma((3, dps)),
            dma((peers,)), dma((peers,)), dma((peers,)), dma((peers,)),
            dma, dma((radial,)), dma((radial,)),
        ],
        compiler_params=pltpu.CompilerParams(
            vmem_limit_bytes=VMEM_LIMIT, collective_id=0, has_side_effects=True
        ),
    )(inputs[0], weight, bias[None], cotangent[0])
    row_in = pl.BlockSpec((1, azimuth, channels, axial), lambda r: (r, 0, 0, 0))
    row_out = pl.BlockSpec((channels, 1, azimuth, axial), lambda r: (0, r, 0, 0))
    weight_spec = pl.BlockSpec((rows, depth), lambda r: (0, 0))
    bias_spec = pl.BlockSpec((1, rows), lambda r: (0, 0))
    output, input_grad, weight_grad, bias_grad = pl.pallas_call(
        turn_kernel,
        grid=(radial,),
        out_shape=(
            shape((outs, radial, azimuth, axial), BF16),
            shape((channels, radial, azimuth, axial), BF16),
            shape((rows, depth), F32),
            shape((1, rows), F32),
        ),
        in_specs=[row_in, row_in, weight_spec, bias_spec],
        out_specs=(row_out, row_out, weight_spec, bias_spec),
        compiler_params=pltpu.CompilerParams(vmem_limit_bytes=63 * 1024 * 1024),
    )(output, input_grad, weight_grad, bias_grad)
    return output[None], input_grad[None], weight_grad, bias_grad[0]


def solution(mesh):
    field_spec = P("dp", None, "rad", "azi", None)
    return jax.shard_map(
        on_device,
        mesh=mesh,
        in_specs=(field_spec, P("dp", None), P("dp"), field_spec),
        out_specs=(field_spec, field_spec, P("dp", None), P("dp")),
        check_vma=False,
    )
```
